128 devices in a mesh: groups: 32 (over y, x, core), block: 4 (over z).
Axes of the slice: x: 4, y: 4, z: 4, core: 2. Of those that a mesh axis runs over, the one named last changes fastest.
Arguments:
- embeddings: bfloat16 [65536, 768], P(('groups', 'block'))
- cluster_ids: int32 [65536], P(('groups', 'block')), may hold values from 0 to 511, as said below
Outputs:
- similarity: float32 [65536], P(('groups', 'block'))
The draws below stay inside these ranges and needn't reach their ends.
Inputs may be any that keep to these rules, and one draw needn't show every extreme that they name: `cluster_ids`: clusters 16 * g to 16 * g + 15 form owner group g. Among the 512 rows of one device at most 64 lie in one group's clusters, and one group gets exactly 64 rows from every device.
All inputs are finite; a program needn't handle non-finite values.
Results may differ from the reference program's by a relative error of at most 0.00053.
Values may be sent and summed in bfloat16 or wider, within the bound.
No kernel may reach another device: no remote copies, remote signals or barrier semaphores. Data moves between devices by JAX's collectives and lax.ppermute only.
A program may use at most 64 MiB of HBM per device.

```python
import jax
import jax.numpy as jnp
from jax import lax

D = 768
TOK_DEV = 512
CL_GRP = 16
TOKENS = 65536
CLUSTERS = 512
CAP = 64
N_GROUPS = 32
N_BLOCK = 4


def cluster_layout(key):
    level_key, heavy_key, jitter_key, order_key, pick_key, second_key = jax.random.split(key, 6)
    devices = N_GROUPS * N_BLOCK
    capacity = 4 * TOK_DEV // N_GROUPS
    levels = jax.random.randint(level_key, (N_GROUPS,), 0, 4)
    stride = jnp.left_shift(jnp.ones_like(levels), levels)
    heavy = jax.random.randint(heavy_key, (), 0, N_GROUPS)
    jitter = jax.random.randint(jitter_key, (devices, N_GROUPS, capacity), 0, 32)
    depth = jnp.arange(capacity, dtype=jnp.int32)
    scored = depth[None, None, :] * stride[None, :, None] * 32 + jitter
    forced = jnp.arange(N_GROUPS, dtype=jnp.int32)[None, :, None] == heavy
    scored = jnp.where(forced, depth[None, None, :] - capacity, scored)
    flat_index = jnp.arange(N_GROUPS * capacity, dtype=jnp.int32)
    ranked = scored.reshape(devices, N_GROUPS * capacity) * (N_GROUPS * capacity) + flat_index[None, :]
    chosen = jnp.argsort(ranked, axis=1)[:, :TOK_DEV]
    shuffle = jax.random.randint(order_key, (devices, TOK_DEV), 0, 1 << 20) * TOK_DEV + jnp.arange(TOK_DEV, dtype=jnp.int32)[None, :]
    chosen = jnp.take_along_axis(chosen, jnp.argsort(shuffle, axis=1), axis=1)
    group_of = chosen // capacity
    inner = jnp.minimum(jax.random.randint(pick_key, (devices, TOK_DEV), 0, CL_GRP), jax.random.randint(second_key, (devices, TOK_DEV), 0, CL_GRP))
    return (group_of * CL_GRP + inner).reshape(-1).astype(jnp.int32)


def draw_cluster_ids(key, part):
    return cluster_layout(key)


def draw_embeddings(key, part):
    clusters = cluster_layout(key)
    key = jax.random.fold_in(key, 7)
    center_key, noise_key, scale_key = jax.random.split(key, 3)
    centers = jax.random.normal(center_key, (CLUSTERS, D), jnp.float32)
    picked = centers[clusters]
    noise = jax.random.normal(noise_key, (TOKENS, D), jnp.float32)
    mixed = picked + noise
    scales = jnp.exp(jax.random.uniform(scale_key, (TOKENS, 1), jnp.float32, -1.2, 1.1))
    return (mixed * scales).astype(jnp.bfloat16)


def setup_inputs(seed: int = 0) -> dict:
    key_of = jax.random.split(jax.random.key(seed), 3)
    return {
        "embeddings": draw_embeddings(jax.random.fold_in(key_of[2], 71), 0),
        "cluster_ids": draw_cluster_ids(jax.random.fold_in(key_of[2], 71), 0),
    }


def reference(embeddings, cluster_ids):
    widened = embeddings.astype(jnp.float32)
    normed = (widened * lax.rsqrt(lax.optimization_barrier(jnp.sum(widened * widened, axis=1, keepdims=True)) + 1e-06)).astype(jnp.bfloat16)
    float_rows = normed.astype(jnp.float32)
    devices = N_GROUPS * N_BLOCK
    owner_group = cluster_ids // CL_GRP
    by_device = owner_group.reshape(devices, TOK_DEV)
    one_hot = (by_device[:, :, None] == jnp.arange(N_GROUPS, dtype=jnp.int32)[None, None, :]).astype(jnp.int32)
    slot_index = lax.optimization_barrier(jnp.sum(jnp.cumsum(one_hot, axis=1) * one_hot, axis=2)) - 1
    source_dev = jnp.arange(devices, dtype=jnp.int32)[:, None]
    position = (source_dev * CAP + slot_index).reshape(-1).astype(jnp.int32)
    table = jnp.full((N_GROUPS, devices * CAP), -1, jnp.int32)
    table = table.at[owner_group, position].set(jnp.arange(TOKENS, dtype=jnp.int32))

    def per_group(row_index):
        valid_row = row_index >= 0
        safe_index = jnp.maximum(row_index, 0)
        group_rows = float_rows[safe_index]
        group_ids = jnp.where(valid_row, cluster_ids[safe_index], -1)
        total_rows = group_rows.shape[0]
        block_rows = min(512, total_rows)
        all_pos = jnp.arange(total_rows, dtype=jnp.int32)

        def per_block(block_index):
            first_row = block_index * block_rows
            left_rows = lax.dynamic_slice_in_dim(group_rows, first_row, block_rows, 0)
            left_ids = lax.dynamic_slice_in_dim(group_ids, first_row, block_rows, 0)
            left_pos = first_row + jnp.arange(block_rows, dtype=jnp.int32)
            scores = jnp.dot(left_rows, group_rows.T, precision=lax.Precision.HIGHEST)
            matches = (left_ids[:, None] == group_ids[None, :]) & (left_ids[:, None] >= 0) & (left_pos[:, None] != all_pos[None, :])
            return lax.optimization_barrier(jnp.max(jnp.where(matches, scores, -1.0), axis=1))
        return lax.map(per_block, jnp.arange(total_rows // block_rows, dtype=jnp.int32)).reshape(-1)
    best_table = lax.map(per_group, table)
    return best_table[owner_group, position]
```

```python
import functools
from typing import NamedTuple

import jax
import jax.numpy as jnp
import numpy as np
from jax import lax
from jax.experimental import pallas as pl
from jax.experimental.pallas import tpu as pltpu
from jax.sharding import Mesh
from jax.sharding import PartitionSpec as P

CL_GRP = 16
GROUPS = 32
GROUP_CAP = 64
WIDTH = 768
ROWS = 512
CHIPS = 64
KINDS = 4
TAIL = 16
FEATURES = 128
WIDE = WIDTH + FEATURES
LANES = 128
ALIGN = 16
COLS = 256
SAME = 4.0
HEAVY_LOAD = 72

F32 = jnp.float32
BF16 = jnp.bfloat16
I32 = jnp.int32


class Plan(NamedTuple):
    slots: int
    shift: tuple
    chunk: int
    capacity: int
    step: int
    sized: bool

    @property
    def held(self):
        return CHIPS * self.slots

    def reach(self, row):
        return row // (self.chunk // self.slots * (self.slots - 1)) * self.chunk

    def block_of(self, lane):
        return (lane * self.shift[0]) >> self.shift[1]

    def slot_of(self, lane):
        return lane - self.slots * self.block_of(lane)

    def first_lane(self):
        return self.slots * (lax.axis_index("yx") * 4 + lax.axis_index("z"))


TIGHT = Plan(24, (2731, 16), 384, 768, 384, True)
ROOMY = Plan(32, (1, 5), 256, 1280, 320, False)


def iota(shape, dim):
    return lax.broadcasted_iota(I32, shape, dim)


def deal(plan, group_hit):
    count = jnp.sum(group_hit, axis=1, keepdims=True)
    count_row = lax.dot_general(
        jnp.ones((8, ROWS), BF16),
        group_hit.astype(BF16),
        (((1,), (1,)), ((), ())),
        preferred_element_type=F32,
    )[:1]
    index = iota((GROUPS, 1), 0)
    index_row = iota((1, GROUPS), 1)
    full = (count == GROUP_CAP).astype(F32)
    heavy = jnp.sum(full * index.astype(F32), axis=0, keepdims=True).astype(I32)
    unsure = jnp.sum(full, axis=0, keepdims=True) != 1.0
    top = jnp.max(jnp.where(index == heavy, 0.0, count), axis=0, keepdims=True)

    def size_class(sizes, where):
        if plan.sized:
            value = (
                (10 * sizes > 7 * top).astype(I32)
                + (20 * sizes > 7 * top).astype(I32)
                + (50 * sizes > 9 * top).astype(I32)
            )
        else:
            value = jnp.zeros(sizes.shape, I32)
        return jnp.where(where == heavy, -1, value)

    mine = size_class(count, index)
    theirs = size_class(count_row, index_row)
    ahead = (theirs > mine) | ((theirs == mine) & (index_row < index))
    order = jnp.sum(ahead.astype(F32), axis=1, keepdims=True).astype(I32)
    ends = [jnp.sum((mine >= least).astype(F32)).astype(I32) for least in (3, 2, 1)]
    loads = [jnp.int32(0), jnp.int32(0), jnp.int32(0), jnp.int32(HEAVY_LOAD)]
    taken = [jnp.int32(0), jnp.int32(0), jnp.int32(0), jnp.int32(1)]
    code = jnp.full((GROUPS, 1), 3 * 32, I32)
    for turn in range(GROUPS - 1):
        if plan.sized:
            weight = jnp.where(
                turn < ends[0], 32, jnp.where(turn < ends[1], 16, jnp.where(turn < ends[2], 8, 4))
            )
        else:
            weight = jnp.int32(14)
        least, kind = loads[0], jnp.int32(0)
        place = taken[0]
        for other in range(1, KINDS):
            better = loads[other] < least
            least = jnp.where(better, loads[other], least)
            kind = jnp.where(better, other, kind)
            place = jnp.where(better, taken[other], place)
        for other in range(KINDS):
            chosen = kind == other
            loads[other] = loads[other] + jnp.where(chosen, weight, 0)
            taken[other] = taken[other] + jnp.where(chosen, 1, 0)
        code = jnp.where(order == turn, kind * 32 + place, code)
    return code, unsure


def send_kernel(plan, ids_ref, rows_ref, out_ref, where_ref, my_ids, my_rows, arrived):
    fetch_ids = pltpu.make_async_copy(ids_ref, my_ids, arrived.at[0])
    fetch_rows = pltpu.make_async_copy(rows_ref, my_rows, arrived.at[1])
    fetch_ids.start()
    fetch_rows.start()
    fetch_ids.wait()
    ids = my_ids[...]
    inner = ids & 15
    hit = iota((GROUPS, ROWS), 0) == (ids >> 4)
    code_of_group, unsure = deal(plan, hit.astype(F32))
    code_of_group = code_of_group.astype(F32)
    code = jnp.sum(jnp.where(hit, code_of_group, 0.0), axis=0, keepdims=True).astype(I32)
    kind, place = code >> 5, code & 31
    odd = (place & 1) == 1
    turned_in_last = (place > 0) & ((place < 4) | odd)
    turned_elsewhere = ((place + 1) & 2) == 2
    in_last = kind == KINDS - 1
    turned = (in_last & turned_in_last) | (~in_last & turned_elsewhere)
    chip = kind * 16 + jnp.where(turned, 15 - inner, inner)

    to_chip = (iota((CHIPS, ROWS), 0) == chip).astype(F32)
    earlier = (iota((ROWS, ROWS), 0) < iota((ROWS, ROWS), 1)).astype(BF16)
    rank = jnp.dot(to_chip.astype(BF16), earlier, preferred_element_type=F32)
    slot = jnp.sum(to_chip * rank, axis=0, keepdims=True).astype(I32)
    over = slot >= plan.slots - 1
    flat = jnp.where(over, -1, chip * plan.slots + slot)
    lane = jnp.where(over, -1, (plan.first_lane() + slot) & (LANES - 1))
    where_ref[...] = jnp.concatenate([chip, lane, jnp.zeros((6, ROWS), I32)], axis=0)
    lost = jnp.max(over.astype(F32), axis=1, keepdims=True)
    flag = jnp.maximum(lost, unsure.astype(F32))

    fetch_rows.wait()
    wide = my_rows[...].astype(F32)
    scale = lax.rsqrt(jnp.sum(wide * wide, axis=1, keepdims=True) + 1e-6)
    normed = (wide * scale).astype(BF16)

    at_lane = (iota((LANES, ROWS), 0) == lane).astype(BF16)
    tagged = (to_chip * (place + 1).astype(F32)).astype(BF16)
    tags = lax.dot_general(tagged, at_lane, (((1,), (1,)), ((), ())), preferred_element_type=F32)
    shown = iota((GROUPS, 128), 1) == iota((GROUPS, 128), 0) + 32
    note = jnp.sum(jnp.where(shown, code_of_group, 0.0), axis=0, keepdims=True)
    note = jnp.where(iota((1, 128), 1) == 0, flag, note)
    meta = jnp.concatenate([tags, jnp.broadcast_to(note, (CHIPS, LANES))], axis=1)
    blocks = plan.chunk // plan.slots
    for first in range(0, plan.held, plan.chunk):
        row = iota((plan.chunk, ROWS), 0) + first
        out = jnp.dot((row == flat).astype(BF16), normed, preferred_element_type=F32)
        noted = []
        for block in range(blocks):
            end = (block + 1) * plan.slots
            chip_meta = meta[first // plan.slots + block, :][None, :]
            last = jnp.where(iota((8, 2 * LANES), 0) == 7, chip_meta, 0.0)
            noted.append(out[end - plan.slots : end - 8, : 2 * LANES])
            noted.append(out[end - 8 : end, : 2 * LANES] + last)
        noted = jnp.concatenate(noted, axis=0)
        out = jnp.concatenate([noted, out[:, 2 * LANES :]], axis=1)
        out_ref[pl.ds(first, plan.chunk), :] = out.astype(BF16)


def compact_kernel(plan, held_ref, out_ref, pos_ref, total_ref):
    held = plan.held
    rows = []
    for source in range(CHIPS):
        at = (source + 1) * plan.slots - 1
        tile = held_ref[pl.ds(at // 16 * 16, 16), : 2 * LANES].astype(F32)
        rows.append(tile[at % 16 : at % 16 + 1])
    meta = jnp.concatenate(rows, axis=0)
    tags = meta[:, :LANES]
    note_top = jnp.max(meta[:, LANES:], axis=0, keepdims=True)
    note_low = jnp.min(meta[:, LANES:], axis=0, keepdims=True)
    note_lane = iota((1, 128), 1)
    flag = jnp.max(
        jnp.where(note_lane == 0, note_top, jnp.where(note_lane >= 32, note_top - note_low, 0.0))
    )
    count = jnp.sum((tags > 0).astype(F32), axis=1, keepdims=True)
    before = (iota((CHIPS, CHIPS), 1) < iota((CHIPS, CHIPS), 0)).astype(BF16)
    offset = jnp.dot(
        before, jnp.broadcast_to(count, (CHIPS, 128)).astype(BF16), preferred_element_type=F32
    )[:, :1]
    own_block = plan.block_of(iota((CHIPS, held), 1)) == iota((CHIPS, held), 0)
    tag_row = jnp.sum(
        jnp.where(own_block, jnp.concatenate([tags] * (held // LANES), axis=1), 0.0),
        axis=0,
        keepdims=True,
    )
    offset_row = jnp.sum(jnp.where(own_block, offset, 0.0), axis=0, keepdims=True).astype(I32)
    pos = jnp.where(tag_row > 0, offset_row + plan.slot_of(iota((1, held), 1)), -1)
    pos_ref[...] = jnp.broadcast_to(pos, (8, held))
    total = jnp.sum(count).astype(I32)
    source = iota((CHIPS, 1), 0)
    total_ref[pl.ds(0, ALIGN), :] = jnp.zeros((ALIGN, WIDE), BF16)
    base = 0
    chunk = plan.chunk
    for first in range(0, held, chunk):
        if first:
            low = jnp.sum(jnp.where(source == first // plan.slots, offset, 0.0)).astype(I32)
            base = pl.multiple_of((low >> 4) << 4, ALIGN)
        lanes = slice(first, first + chunk)
        take = (iota((chunk + ALIGN, chunk), 0) + base) == pos[:, lanes]
        part = jnp.dot(take.astype(BF16), held_ref[lanes, :], preferred_element_type=F32)
        tag = jnp.sum(jnp.where(take, tag_row[:, lanes], 0.0), axis=1, keepdims=True).astype(I32)
        feature = jnp.where(iota((chunk + ALIGN, FEATURES), 1) == tag - 1, 2.0, 0.0)
        part = part.astype(BF16)
        feature = feature.astype(BF16)
        head, rest = pl.ds(base, ALIGN), pl.ds(base + ALIGN, chunk)
        total_ref[head, :WIDTH] += part[:ALIGN]
        total_ref[rest, :WIDTH] = part[ALIGN:]
        total_ref[head, WIDTH:] += feature[:ALIGN]
        total_ref[rest, WIDTH:] = feature[ALIGN:]

    def clear(tile, carry):
        rows = pl.ds(pl.multiple_of(tile * ALIGN, ALIGN), ALIGN)
        total_ref[rows, :] = jnp.zeros((ALIGN, WIDE), BF16)
        return carry

    lax.fori_loop((base + chunk + ALIGN) >> 4, plan.capacity // ALIGN, clear, 0)
    out_ref[pl.ds(0, plan.capacity), :] = total_ref[pl.ds(0, plan.capacity), :]
    flag = jnp.maximum(flag, (total > plan.capacity).astype(F32))
    note = jnp.where(note_lane == 0, flag, jnp.where(note_lane >= 32, note_top, 0.0))
    tail = jnp.concatenate([note, jnp.zeros((1, WIDE - 128), F32)], axis=1)
    out_ref[pl.ds(plan.capacity, TAIL), :] = jnp.broadcast_to(tail, (TAIL, WIDE)).astype(BF16)


def score_block(plan, own_ref, rows_ref, start, best, same):
    own = own_ref[pl.ds(start, COLS), :]
    for first in range(0, plan.capacity, plan.step):
        rows = rows_ref[pl.ds(first, plan.step), :]
        scores = lax.dot_general(
            rows, own, (((1,), (1,)), ((), ())), preferred_element_type=F32
        )
        if same:
            row_index = iota((plan.step, COLS), 0) + first
            scores = jnp.where(row_index == iota((plan.step, COLS), 1) + start, -1.0, scores)
        best = jnp.maximum(best, jnp.max(scores.reshape(plan.step // 8, 8, COLS), axis=0))
    return best


def own_kernel(plan, own_ref, out_ref):
    for start in range(0, plan.capacity, COLS):
        best = jnp.full((8, COLS), -1.0, F32)
        out_ref[:, pl.ds(start, COLS)] = score_block(plan, own_ref, own_ref, start, best, True)


def other_kernel(
    plan, pos_ref, own_ref, other_ref, part_ref, out_ref
):
    own_note = own_ref[pl.ds(plan.capacity, TAIL), :128].astype(F32)
    other_note = other_ref[pl.ds(plan.capacity, TAIL), :128].astype(F32)
    note_lane = iota((TAIL, 128), 1)
    differs = (note_lane >= 32) & (own_note != other_note)
    raised = jnp.where(note_lane == 0, jnp.maximum(own_note, other_note), 0.0)
    flag = jnp.max(jnp.where(differs, 1.0, raised))
    found = [jnp.zeros((8, plan.chunk), F32)] * (plan.held // plan.chunk)
    for start in range(0, plan.capacity, COLS):
        best = score_block(plan, own_ref, other_ref, start, part_ref[:, pl.ds(start, COLS)], False)
        top = jnp.max(jnp.transpose(best), axis=1, keepdims=True) - SAME
        top = jnp.maximum(top, -1.0)
        row = iota((COLS, plan.chunk), 0) + start
        for index in range(plan.reach(start) // plan.chunk, plan.held // plan.chunk):
            pos = pos_ref[0:1, index * plan.chunk : (index + 1) * plan.chunk]
            value = jnp.where(row == pos, top, 0.0)
            found[index] += jnp.sum(value.reshape(COLS // 8, 8, plan.chunk), axis=0)

    blocks = plan.chunk // plan.slots
    for index, values in enumerate(found):
        lane = iota((1, plan.chunk), 1)
        values = jnp.sum(values, axis=0, keepdims=True)
        values = jnp.where(plan.slot_of(lane) == plan.slots - 1, flag, values)
        in_block = plan.block_of(lane) == iota((blocks, plan.chunk), 0)
        mine = jnp.where(in_block, values, 0.0)
        folded = mine[:, :LANES]
        for first in range(LANES, plan.chunk, LANES):
            folded = folded + mine[:, first : first + LANES]
        out_ref[index * blocks : (index + 1) * blocks, :] = folded


def answer_kernel(plan, where_ref, back_ref, out_ref, flag_ref):
    chip = where_ref[0:1, :]
    lane = where_ref[1:2, :]
    back = back_ref[...]
    to_chip = (iota((CHIPS, ROWS), 0) == chip).astype(F32)
    by_row = lax.dot_general(
        back,
        to_chip,
        (((0,), (0,)), ((), ())),
        preferred_element_type=F32,
        precision=lax.Precision.HIGHEST,
    )
    at_lane = iota((LANES, ROWS), 0) == lane
    out_ref[...] = jnp.sum(jnp.where(at_lane, by_row, 0.0), axis=0, keepdims=True)
    last = iota((CHIPS, LANES), 1) == ((plan.first_lane() + plan.slots - 1) & (LANES - 1))
    flag_ref[0] = (jnp.max(jnp.where(last, back, 0.0)) > 0.0).astype(I32)


VMEM = pl.BlockSpec(memory_space=pltpu.VMEM)
SMEM = pl.BlockSpec(memory_space=pltpu.SMEM)
HBM = pl.BlockSpec(memory_space=pltpu.HBM)


def shape(dims, dtype):
    return jax.ShapeDtypeStruct(dims, dtype)


def call(kernel, plan, name, **options):
    return pl.pallas_call(
        functools.partial(kernel, plan),
        compiler_params=pltpu.CompilerParams(vmem_limit_bytes=48 * 1024 * 1024),
        name=name,
        **options,
    )


def swap(plan, message):
    return lax.all_to_all(message, ("yx", "z"), split_axis=0, concat_axis=0, tiled=True)


def owner_path(plan, embeddings, cluster_ids):
    message, where = call(
        send_kernel,
        plan,
        "send",
        out_shape=(shape((plan.held, WIDTH), BF16), shape((8, ROWS), I32)),
        in_specs=[HBM, HBM],
        out_specs=(VMEM, VMEM),
        scratch_shapes=[
            pltpu.VMEM((1, ROWS), I32),
            pltpu.VMEM((ROWS, WIDTH), BF16),
            pltpu.SemaphoreType.DMA((2,)),
        ],
    )(cluster_ids.reshape(1, ROWS), embeddings)
    held = swap(plan, message)
    packed, pos = call(
        compact_kernel,
        plan,
        "compact",
        out_shape=(
            shape((plan.capacity + TAIL, WIDE), BF16),
            shape((8, plan.held), I32),
        ),
        in_specs=[VMEM],
        out_specs=(VMEM, VMEM),
        scratch_shapes=[pltpu.VMEM((plan.held + plan.chunk + ALIGN, WIDE), BF16)],
    )(held)
    other = lax.ppermute(packed, "core", [(0, 1), (1, 0)])
    part = call(
        own_kernel,
        plan,
        "score_own",
        out_shape=shape((8, plan.capacity), F32),
        in_specs=[VMEM],
        out_specs=VMEM,
        cost_estimate=pl.CostEstimate(
            flops=2 * plan.capacity**2 * WIDE,
            bytes_accessed=2 * plan.capacity * WIDE,
            transcendentals=0,
        ),
    )(packed)
    best = call(
        other_kernel,
        plan,
        "score_other",
        out_shape=shape((CHIPS, LANES), F32),
        in_specs=[VMEM, VMEM, VMEM, VMEM],
        out_specs=VMEM,
    )(pos, packed, other, part)
    back = swap(plan, best)
    answer, flag = call(
        answer_kernel,
        plan,
        "answer",
        out_shape=(shape((1, ROWS), F32), shape((1,), I32)),
        in_specs=[VMEM, VMEM],
        out_specs=(VMEM, SMEM),
    )(where, back)
    return answer.reshape(ROWS), flag[0]


def pair_max(left_rows, left_ids, left_pos, right_rows, right_ids, right_pos):
    left_total, width = left_rows.shape
    left_step = min(512, left_total)
    left_count = left_total // left_step

    def left_turn(carry, left_tuple):
        part_rows, part_ids, part_pos = left_tuple
        scores = lax.dot_general(
            part_rows, right_rows, (((1,), (1,)), ((), ())), preferred_element_type=F32
        )
        matches = (
            (part_ids[:, None] == right_ids[None, :])
            & (part_ids[:, None] >= 0)
            & (part_pos[:, None] != right_pos[None, :])
        )
        return carry, jnp.max(jnp.where(matches, scores, -1.0), axis=1)

    _, row_best = lax.scan(
        left_turn,
        0,
        (
            left_rows.reshape(left_count, left_step, width),
            left_ids.reshape(left_count, left_step),
            left_pos.reshape(left_count, left_step),
        ),
    )
    return row_best.reshape(-1)


def gather(piece):
    copies = jnp.broadcast_to(piece[None], (4, *piece.shape))
    whole = lax.all_to_all(copies, "z", split_axis=0, concat_axis=0, tiled=True)
    return whole.reshape(-1, *piece.shape[1:])


def any_path(embeddings, cluster_ids):
    axes = ("yx", "core")
    widened = embeddings.astype(F32)
    normed = (
        widened * lax.rsqrt(jnp.sum(widened * widened, axis=1, keepdims=True) + 1e-06)
    ).astype(BF16)
    owner_group = cluster_ids // CL_GRP
    one_hot = (owner_group[:, None] == jnp.arange(GROUPS, dtype=I32)[None, :]).astype(I32)
    slot_index = jnp.sum(jnp.cumsum(one_hot, axis=0) * one_hot, axis=1) - 1
    flat_slot = owner_group * GROUP_CAP + slot_index
    total = GROUPS * GROUP_CAP
    placement = jnp.arange(total, dtype=I32)[:, None] == flat_slot[None, :]
    outgoing = jnp.dot(placement.astype(BF16), normed, preferred_element_type=F32).astype(BF16)
    outgoing = outgoing.reshape(GROUPS, GROUP_CAP, WIDTH)
    outgoing_ids = jnp.max(jnp.where(placement, cluster_ids[None, :], -1), axis=1)
    outgoing_ids = outgoing_ids.reshape(GROUPS, GROUP_CAP)
    received = lax.all_to_all(outgoing, axes, 0, 0, tiled=True).reshape(total, WIDTH)
    received_ids = lax.all_to_all(outgoing_ids, axes, 0, 0, tiled=True).reshape(total)
    own_pos = jnp.arange(total, dtype=I32) + lax.axis_index("z") * total
    piece_rows = gather(received)
    piece_ids = gather(received_ids)
    piece_pos = jnp.arange(piece_rows.shape[0], dtype=I32)
    best = pair_max(received, received_ids, own_pos, piece_rows, piece_ids, piece_pos)
    best = jnp.maximum(best, -1.0)
    returned = lax.all_to_all(best.reshape(GROUPS, GROUP_CAP), axes, 0, 0, tiled=True)
    return jnp.max(jnp.where(placement, returned.reshape(total)[:, None], -2.0), axis=0)


def body(embeddings, cluster_ids):
    def keep(rows, ids, done):
        return done

    def last_resort(rows, ids, done):
        return any_path(rows, ids)

    def roomy(rows, ids, done):
        answer, flag = owner_path(ROOMY, rows, ids)
        return lax.switch(flag, [keep, last_resort], rows, ids, answer)

    answer, flag = owner_path(TIGHT, embeddings, cluster_ids)
    return lax.switch(flag, [keep, roomy], embeddings, cluster_ids, answer)


def solution(mesh):
    chips = Mesh(np.asarray(mesh.devices).reshape(16, 2, 4), ("yx", "core", "z"))
    axes = ("yx", "core", "z")
    return jax.shard_map(
        body, mesh=chips, in_specs=(P(axes, None), P(axes)), out_specs=P(axes), check_vma=False
    )
```

```python
import functools
from typing import NamedTuple

import jax
import jax.numpy as jnp
import numpy as np
from jax import lax
from jax.experimental import pallas as pl
from jax.experimental.pallas import tpu as pltpu
from jax.sharding import Mesh
from jax.sharding import PartitionSpec as P

CL_GRP = 16
GROUPS = 32
GROUP_CAP = 64
WIDTH = 768
ROWS = 512
CHIPS = 64
KINDS = 4
TAIL = 16
LANES = 128
ALIGN = 16
COLS = 256
HEAVY_LOAD = 72

F32 = jnp.float32
BF16 = jnp.bfloat16
I32 = jnp.int32


class Plan(NamedTuple):
    slots: int
    shift: tuple
    chunk: int
    capacity: int
    step: int
    sized: bool

    @property
    def held(self):
        return CHIPS * self.slots

    @property
    def tail(self):
        return -(-self.capacity // WIDTH) * TAIL

    def reach(self, row):
        return row // (self.chunk // self.slots * (self.slots - 1)) * self.chunk

    def block_of(self, lane):
        return (lane * self.shift[0]) >> self.shift[1]

    def slot_of(self, lane):
        return lane - self.slots * self.block_of(lane)

    def first_lane(self):
        return self.slots * (lax.axis_index("yx") * 4 + lax.axis_index("z"))


TIGHT = Plan(24, (2731, 16), 384, 768, 384, True)
ROOMY = Plan(32, (1, 5), 256, 1280, 320, False)


def iota(shape, dim):
    return lax.broadcasted_iota(I32, shape, dim)


def deal(plan, group_hit):
    count = jnp.sum(group_hit, axis=1, keepdims=True)
    count_row = lax.dot_general(
        jnp.ones((8, ROWS), BF16),
        group_hit.astype(BF16),
        (((1,), (1,)), ((), ())),
        preferred_element_type=F32,
    )[:1]
    index = iota((GROUPS, 1), 0)
    index_row = iota((1, GROUPS), 1)
    full = (count == GROUP_CAP).astype(F32)
    heavy = jnp.sum(full * index.astype(F32), axis=0, keepdims=True).astype(I32)
    unsure = jnp.sum(full, axis=0, keepdims=True) != 1.0
    top = jnp.max(jnp.where(index == heavy, 0.0, count), axis=0, keepdims=True)

    def size_class(sizes, where):
        if plan.sized:
            value = (
                (10 * sizes > 7 * top).astype(I32)
                + (20 * sizes > 7 * top).astype(I32)
                + (50 * sizes > 9 * top).astype(I32)
            )
        else:
            value = jnp.zeros(sizes.shape, I32)
        return jnp.where(where == heavy, -1, value)

    mine = size_class(count, index)
    theirs = size_class(count_row, index_row)
    ahead = (theirs > mine) | ((theirs == mine) & (index_row < index))
    order = jnp.sum(ahead.astype(F32), axis=1, keepdims=True).astype(I32)
    ends = [jnp.sum((mine >= least).astype(F32)).astype(I32) for least in (3, 2, 1)]
    loads = [jnp.int32(0), jnp.int32(0), jnp.int32(0), jnp.int32(HEAVY_LOAD)]
    taken = [jnp.int32(0), jnp.int32(0), jnp.int32(0), jnp.int32(1)]
    code = jnp.full((GROUPS, 1), 3 * 32, I32)
    for turn in range(GROUPS - 1):
        if plan.sized:
            weight = jnp.where(
                turn < ends[0], 32, jnp.where(turn < ends[1], 16, jnp.where(turn < ends[2], 8, 4))
            )
        else:
            weight = jnp.int32(14)
        least, kind = loads[0], jnp.int32(0)
        place = taken[0]
        for other in range(1, KINDS):
            better = loads[other] < least
            least = jnp.where(better, loads[other], least)
            kind = jnp.where(better, other, kind)
            place = jnp.where(better, taken[other], place)
        for other in range(KINDS):
            chosen = kind == other
            loads[other] = loads[other] + jnp.where(chosen, weight, 0)
            taken[other] = taken[other] + jnp.where(chosen, 1, 0)
        code = jnp.where(order == turn, kind * 32 + place, code)
    return code, unsure


def send_kernel(plan, ids_ref, rows_ref, out_ref, where_ref, my_ids, my_rows, arrived):
    fetch_ids = pltpu.make_async_copy(ids_ref, my_ids, arrived.at[0])
    fetch_rows = pltpu.make_async_copy(rows_ref, my_rows, arrived.at[1])
    fetch_ids.start()
    fetch_rows.start()
    fetch_ids.wait()
    ids = my_ids[...]
    inner = ids & 15
    hit = iota((GROUPS, ROWS), 0) == (ids >> 4)
    code_of_group, unsure = deal(plan, hit.astype(F32))
    code_of_group = code_of_group.astype(F32)
    code = jnp.sum(jnp.where(hit, code_of_group, 0.0), axis=0, keepdims=True).astype(I32)
    kind, place = code >> 5, code & 31
    odd = (place & 1) == 1
    turned_in_last = (place > 0) & ((place < 4) | odd)
    turned_elsewhere = ((place + 1) & 2) == 2
    in_last = kind == KINDS - 1
    turned = (in_last & turned_in_last) | (~in_last & turned_elsewhere)
    chip = kind * 16 + jnp.where(turned, 15 - inner, inner)

    to_chip = (iota((CHIPS, ROWS), 0) == chip).astype(F32)
    earlier = (iota((ROWS, ROWS), 0) < iota((ROWS, ROWS), 1)).astype(BF16)
    rank = jnp.dot(to_chip.astype(BF16), earlier, preferred_element_type=F32)
    slot = jnp.sum(to_chip * rank, axis=0, keepdims=True).astype(I32)
    over = slot >= plan.slots - 1
    flat = jnp.where(over, -1, chip * plan.slots + slot)
    lane = jnp.where(over, -1, (plan.first_lane() + slot) & (LANES - 1))
    where_ref[...] = jnp.concatenate([chip, lane, jnp.zeros((6, ROWS), I32)], axis=0)
    lost = jnp.max(over.astype(F32), axis=1, keepdims=True)
    flag = jnp.maximum(lost, unsure.astype(F32))

    fetch_rows.wait()
    wide = my_rows[...].astype(F32)
    scale = lax.rsqrt(jnp.sum(wide * wide, axis=1, keepdims=True) + 1e-6)
    normed = (wide * scale).astype(BF16)

    at_lane = (iota((LANES, ROWS), 0) == lane).astype(BF16)
    tagged = (to_chip * (place + 1).astype(F32)).astype(BF16)
    tags = lax.dot_general(tagged, at_lane, (((1,), (1,)), ((), ())), preferred_element_type=F32)
    shown = iota((GROUPS, 128), 1) == iota((GROUPS, 128), 0) + 32
    note = jnp.sum(jnp.where(shown, code_of_group, 0.0), axis=0, keepdims=True)
    note = jnp.where(iota((1, 128), 1) == 0, flag, note)
    meta = jnp.concatenate([tags, jnp.broadcast_to(note, (CHIPS, LANES))], axis=1)
    blocks = plan.chunk // plan.slots
    for first in range(0, plan.held, plan.chunk):
        row = iota((plan.chunk, ROWS), 0) + first
        out = jnp.dot((row == flat).astype(BF16), normed, preferred_element_type=F32)
        noted = []
        for block in range(blocks):
            end = (block + 1) * plan.slots
            chip_meta = meta[first // plan.slots + block, :][None, :]
            last = jnp.where(iota((8, 2 * LANES), 0) == 7, chip_meta, 0.0)
            noted.append(out[end - plan.slots : end - 8, : 2 * LANES])
            noted.append(out[end - 8 : end, : 2 * LANES] + last)
        noted = jnp.concatenate(noted, axis=0)
        out = jnp.concatenate([noted, out[:, 2 * LANES :]], axis=1)
        out_ref[pl.ds(first, plan.chunk), :] = out.astype(BF16)


def compact_kernel(plan, held_ref, out_ref, tags_ref, pos_ref, total_ref, tag_ref):
    held = plan.held
    rows = []
    for source in range(CHIPS):
        at = (source + 1) * plan.slots - 1
        tile = held_ref[pl.ds(at // 16 * 16, 16), : 2 * LANES].astype(F32)
        rows.append(tile[at % 16 : at % 16 + 1])
    meta = jnp.concatenate(rows, axis=0)
    tags = meta[:, :LANES]
    note_top = jnp.max(meta[:, LANES:], axis=0, keepdims=True)
    note_low = jnp.min(meta[:, LANES:], axis=0, keepdims=True)
    note_lane = iota((1, 128), 1)
    flag = jnp.max(
        jnp.where(note_lane == 0, note_top, jnp.where(note_lane >= 32, note_top - note_low, 0.0))
    )
    count = jnp.sum((tags > 0).astype(F32), axis=1, keepdims=True)
    before = (iota((CHIPS, CHIPS), 1) < iota((CHIPS, CHIPS), 0)).astype(BF16)
    offset = jnp.dot(
        before, jnp.broadcast_to(count, (CHIPS, 128)).astype(BF16), preferred_element_type=F32
    )[:, :1]
    own_block = plan.block_of(iota((CHIPS, held), 1)) == iota((CHIPS, held), 0)
    tag_row = jnp.sum(
        jnp.where(own_block, jnp.concatenate([tags] * (held // LANES), axis=1), 0.0),
        axis=0,
        keepdims=True,
    )
    offset_row = jnp.sum(jnp.where(own_block, offset, 0.0), axis=0, keepdims=True).astype(I32)
    pos = jnp.where(tag_row > 0, offset_row + plan.slot_of(iota((1, held), 1)), -1)
    pos_ref[...] = jnp.broadcast_to(pos, (8, held))
    total = jnp.sum(count).astype(I32)
    source = iota((CHIPS, 1), 0)
    total_ref[pl.ds(0, ALIGN), :] = jnp.zeros((ALIGN, WIDTH), BF16)
    tag_ref[pl.ds(0, ALIGN), :] = jnp.zeros((ALIGN, LANES), BF16)
    base = 0
    chunk = plan.chunk
    for first in range(0, held, chunk):
        if first:
            low = jnp.sum(jnp.where(source == first // plan.slots, offset, 0.0)).astype(I32)
            base = pl.multiple_of((low >> 4) << 4, ALIGN)
        lanes = slice(first, first + chunk)
        take = (iota((chunk + ALIGN, chunk), 0) + base) == pos[:, lanes]
        part = jnp.dot(take.astype(BF16), held_ref[lanes, :], preferred_element_type=F32)
        tag = jnp.sum(jnp.where(take, tag_row[:, lanes], 0.0), axis=1, keepdims=True)
        tag = jnp.broadcast_to(tag, (chunk + ALIGN, LANES)).astype(BF16)
        part = part.astype(BF16)
        head, rest = pl.ds(base, ALIGN), pl.ds(base + ALIGN, chunk)
        total_ref[head, :] += part[:ALIGN]
        total_ref[rest, :] = part[ALIGN:]
        tag_ref[head, :] += tag[:ALIGN]
        tag_ref[rest, :] = tag[ALIGN:]

    def clear(tile, carry):
        rows = pl.ds(pl.multiple_of(tile * ALIGN, ALIGN), ALIGN)
        total_ref[rows, :] = jnp.zeros((ALIGN, WIDTH), BF16)
        tag_ref[rows, :] = jnp.zeros((ALIGN, LANES), BF16)
        return carry

    lax.fori_loop((base + chunk + ALIGN) >> 4, plan.capacity // ALIGN, clear, 0)
    out_ref[pl.ds(0, plan.capacity), :] = total_ref[pl.ds(0, plan.capacity), :]
    tags = tag_ref[pl.ds(0, plan.capacity), :]
    tags_ref[...] = tags
    one_lane = (iota((TAIL, LANES), 1) == 0).astype(BF16)
    tag_lanes = lax.dot_general(
        one_lane, tags, (((1,), (1,)), ((), ())), preferred_element_type=F32
    )
    flag = jnp.maximum(flag, (total > plan.capacity).astype(F32))
    note = jnp.where(note_lane == 0, flag, jnp.where(note_lane >= 32, note_top, 0.0))
    note = jnp.concatenate([note, jnp.zeros((1, plan.capacity - LANES), F32)], axis=1)
    tail = jnp.where(iota((TAIL, plan.capacity), 0) < TAIL // 2, note, tag_lanes)
    for first in range(0, plan.capacity, WIDTH):
        piece = tail[:, first : first + WIDTH].astype(BF16)
        out_ref[pl.ds(plan.capacity + first // WIDTH * TAIL, TAIL), : piece.shape[1]] = piece


def tail_of(plan, ref):
    pieces = []
    for first in range(0, plan.capacity, WIDTH):
        rows = pl.ds(plan.capacity + first // WIDTH * TAIL, TAIL)
        pieces.append(ref[rows, : min(WIDTH, plan.capacity - first)].astype(F32))
    tail = jnp.concatenate(pieces, axis=1)
    return tail[:1, :LANES], tail[TAIL // 2 : TAIL // 2 + 1, :]


def score_block(plan, own_ref, tags_ref, rows_ref, row_tags, start, best, same):
    own = own_ref[pl.ds(start, plan.step), :]
    own_tag = tags_ref[pl.ds(start, plan.step), :1].astype(F32)
    for first in range(0, plan.capacity, COLS):
        rows = rows_ref[pl.ds(first, COLS), :]
        scores = lax.dot_general(
            own, rows, (((1,), (1,)), ((), ())), preferred_element_type=F32
        )
        match = own_tag == row_tags[:, first : first + COLS]
        if same:
            index = iota((plan.step, COLS), 0) + (start - first)
            match = match & (index != iota((plan.step, COLS), 1))
        scores = jnp.where(match, scores, -1.0)
        for lane in range(0, COLS, LANES):
            best = jnp.maximum(best, scores[:, lane : lane + LANES])
    return best


def own_kernel(plan, own_ref, tags_ref, out_ref):
    _, own_tags = tail_of(plan, own_ref)
    for start in range(0, plan.capacity, plan.step):
        best = jnp.full((plan.step, LANES), -1.0, F32)
        best = score_block(plan, own_ref, tags_ref, own_ref, own_tags, start, best, True)
        out_ref[pl.ds(start, plan.step), :] = best


def other_kernel(plan, pos_ref, own_ref, tags_ref, other_ref, part_ref, out_ref):
    own_note, _ = tail_of(plan, own_ref)
    other_note, other_tags = tail_of(plan, other_ref)
    note_lane = iota((1, LANES), 1)
    differs = (note_lane >= 32) & (own_note != other_note)
    raised = jnp.where(note_lane == 0, jnp.maximum(own_note, other_note), 0.0)
    flag = jnp.max(jnp.where(differs, 1.0, raised), axis=1, keepdims=True)
    found = [jnp.zeros((8, plan.chunk), F32)] * (plan.held // plan.chunk)
    for start in range(0, plan.capacity, plan.step):
        best = part_ref[pl.ds(start, plan.step), :]
        best = score_block(plan, own_ref, tags_ref, other_ref, other_tags, start, best, False)
        top = jnp.max(best, axis=1, keepdims=True)
        row = iota((plan.step, plan.chunk), 0) + start
        for index in range(plan.reach(start) // plan.chunk, plan.held // plan.chunk):
            pos = pos_ref[0:1, index * plan.chunk : (index + 1) * plan.chunk]
            value = jnp.where(row == pos, top, 0.0)
            found[index] += jnp.sum(value.reshape(plan.step // 8, 8, plan.chunk), axis=0)

    blocks = plan.chunk // plan.slots
    for index, values in enumerate(found):
        lane = iota((1, plan.chunk), 1)
        values = jnp.sum(values, axis=0, keepdims=True)
        values = jnp.where(plan.slot_of(lane) == plan.slots - 1, flag, values)
        in_block = plan.block_of(lane) == iota((blocks, plan.chunk), 0)
        mine = jnp.where(in_block, values, 0.0)
        folded = mine[:, :LANES]
        for first in range(LANES, plan.chunk, LANES):
            folded = folded + mine[:, first : first + LANES]
        out_ref[index * blocks : (index + 1) * blocks, :] = folded


def answer_kernel(plan, where_ref, back_ref, out_ref, flag_ref):
    chip = where_ref[0:1, :]
    lane = where_ref[1:2, :]
    back = back_ref[...]
    to_chip = (iota((CHIPS, ROWS), 0) == chip).astype(F32)
    by_row = lax.dot_general(
        back,
        to_chip,
        (((0,), (0,)), ((), ())),
        preferred_element_type=F32,
        precision=lax.Precision.HIGHEST,
    )
    at_lane = iota((LANES, ROWS), 0) == lane
    out_ref[...] = jnp.sum(jnp.where(at_lane, by_row, 0.0), axis=0, keepdims=True)
    last = iota((CHIPS, LANES), 1) == ((plan.first_lane() + plan.slots - 1) & (LANES - 1))
    flag_ref[0] = (jnp.max(jnp.where(last, back, 0.0)) > 0.0).astype(I32)


VMEM = pl.BlockSpec(memory_space=pltpu.VMEM)
SMEM = pl.BlockSpec(memory_space=pltpu.SMEM)
HBM = pl.BlockSpec(memory_space=pltpu.HBM)


def shape(dims, dtype):
    return jax.ShapeDtypeStruct(dims, dtype)


def call(kernel, plan, name, **options):
    return pl.pallas_call(
        functools.partial(kernel, plan),
        compiler_params=pltpu.CompilerParams(vmem_limit_bytes=48 * 1024 * 1024),
        name=name,
        **options,
    )


def swap(plan, message):
    return lax.all_to_all(message, ("yx", "z"), split_axis=0, concat_axis=0, tiled=True)


def owner_path(plan, embeddings, cluster_ids):
    message, where = call(
        send_kernel,
        plan,
        "send",
        out_shape=(shape((plan.held, WIDTH), BF16), shape((8, ROWS), I32)),
        in_specs=[HBM, HBM],
        out_specs=(VMEM, VMEM),
        scratch_shapes=[
            pltpu.VMEM((1, ROWS), I32),
            pltpu.VMEM((ROWS, WIDTH), BF16),
            pltpu.SemaphoreType.DMA((2,)),
        ],
    )(cluster_ids.reshape(1, ROWS), embeddings)
    held = swap(plan, message)
    packed, tags, pos = call(
        compact_kernel,
        plan,
        "compact",
        out_shape=(
            shape((plan.capacity + plan.tail, WIDTH), BF16),
            shape((plan.capacity, LANES), BF16),
            shape((8, plan.held), I32),
        ),
        in_specs=[VMEM],
        out_specs=(VMEM, VMEM, VMEM),
        scratch_shapes=[
            pltpu.VMEM((plan.held + plan.chunk + ALIGN, WIDTH), BF16),
            pltpu.VMEM((plan.held + plan.chunk + ALIGN, LANES), BF16),
        ],
    )(held)
    other = lax.ppermute(packed, "core", [(0, 1), (1, 0)])
    part = call(
        own_kernel,
        plan,
        "score_own",
        out_shape=shape((plan.capacity, LANES), F32),
        in_specs=[VMEM, VMEM],
        out_specs=VMEM,
        cost_estimate=pl.CostEstimate(
            flops=2 * plan.capacity**2 * WIDTH,
            bytes_accessed=2 * plan.capacity * WIDTH,
            transcendentals=0,
        ),
    )(packed, tags)
    best = call(
        other_kernel,
        plan,
        "score_other",
        out_shape=shape((CHIPS, LANES), F32),
        in_specs=[VMEM] * 5,
        out_specs=VMEM,
    )(pos, packed, tags, other, part)
    back = swap(plan, best)
    answer, flag = call(
        answer_kernel,
        plan,
        "answer",
        out_shape=(shape((1, ROWS), F32), shape((1,), I32)),
        in_specs=[VMEM, VMEM],
        out_specs=(VMEM, SMEM),
    )(where, back)
    return answer.reshape(ROWS), flag[0]


def pair_max(left_rows, left_ids, left_pos, right_rows, right_ids, right_pos):
    left_total, width = left_rows.shape
    left_step = min(512, left_total)
    left_count = left_total // left_step

    def left_turn(carry, left_tuple):
        part_rows, part_ids, part_pos = left_tuple
        scores = lax.dot_general(
            part_rows, right_rows, (((1,), (1,)), ((), ())), preferred_element_type=F32
        )
        matches = (
            (part_ids[:, None] == right_ids[None, :])
            & (part_ids[:, None] >= 0)
            & (part_pos[:, None] != right_pos[None, :])
        )
        return carry, jnp.max(jnp.where(matches, scores, -1.0), axis=1)

    _, row_best = lax.scan(
        left_turn,
        0,
        (
            left_rows.reshape(left_count, left_step, width),
            left_ids.reshape(left_count, left_step),
            left_pos.reshape(left_count, left_step),
        ),
    )
    return row_best.reshape(-1)


def gather(piece):
    copies = jnp.broadcast_to(piece[None], (4, *piece.shape))
    whole = lax.all_to_all(copies, "z", split_axis=0, concat_axis=0, tiled=True)
    return whole.reshape(-1, *piece.shape[1:])


def any_path(embeddings, cluster_ids):
    axes = ("yx", "core")
    widened = embeddings.astype(F32)
    normed = (
        widened * lax.rsqrt(jnp.sum(widened * widened, axis=1, keepdims=True) + 1e-06)
    ).astype(BF16)
    owner_group = cluster_ids // CL_GRP
    one_hot = (owner_group[:, None] == jnp.arange(GROUPS, dtype=I32)[None, :]).astype(I32)
    slot_index = jnp.sum(jnp.cumsum(one_hot, axis=0) * one_hot, axis=1) - 1
    flat_slot = owner_group * GROUP_CAP + slot_index
    total = GROUPS * GROUP_CAP
    placement = jnp.arange(total, dtype=I32)[:, None] == flat_slot[None, :]
    outgoing = jnp.dot(placement.astype(BF16), normed, preferred_element_type=F32).astype(BF16)
    outgoing = outgoing.reshape(GROUPS, GROUP_CAP, WIDTH)
    outgoing_ids = jnp.max(jnp.where(placement, cluster_ids[None, :], -1), axis=1)
    outgoing_ids = outgoing_ids.reshape(GROUPS, GROUP_CAP)
    received = lax.all_to_all(outgoing, axes, 0, 0, tiled=True).reshape(total, WIDTH)
    received_ids = lax.all_to_all(outgoing_ids, axes, 0, 0, tiled=True).reshape(total)
    own_pos = jnp.arange(total, dtype=I32) + lax.axis_index("z") * total
    piece_rows = gather(received)
    piece_ids = gather(received_ids)
    piece_pos = jnp.arange(piece_rows.shape[0], dtype=I32)
    best = pair_max(received, received_ids, own_pos, piece_rows, piece_ids, piece_pos)
    best = jnp.maximum(best, -1.0)
    returned = lax.all_to_all(best.reshape(GROUPS, GROUP_CAP), axes, 0, 0, tiled=True)
    return jnp.max(jnp.where(placement, returned.reshape(total)[:, None], -2.0), axis=0)


def body(embeddings, cluster_ids):
    def keep(rows, ids, done):
        return done

    def last_resort(rows, ids, done):
        return any_path(rows, ids)

    def roomy(rows, ids, done):
        answer, flag = owner_path(ROOMY, rows, ids)
        return lax.switch(flag, [keep, last_resort], rows, ids, answer)

    answer, flag = owner_path(TIGHT, embeddings, cluster_ids)
    embeddings, cluster_ids, answer, flag = lax.optimization_barrier(
        (embeddings, cluster_ids, answer, flag)
    )
    return lax.switch(flag, [keep, roomy], embeddings, cluster_ids, answer)


def solution(mesh):
    chips = Mesh(np.asarray(mesh.devices).reshape(16, 2, 4), ("yx", "core", "z"))
    axes = ("yx", "core", "z")
    return jax.shard_map(
        body, mesh=chips, in_specs=(P(axes, None), P(axes)), out_specs=P(axes), check_vma=False
    )
```

```python
import functools
from typing import NamedTuple

import jax
import jax.numpy as jnp
import numpy as np
from jax import lax
from jax.experimental import pallas as pl
from jax.experimental.pallas import tpu as pltpu
from jax.sharding import Mesh
from jax.sharding import PartitionSpec as P

CL_GRP = 16
GROUPS = 32
GROUP_CAP = 64
WIDTH = 768
ROWS = 512
CHIPS = 64
KINDS = 4
TAIL = 16
LANES = 128
ALIGN = 16
COLS = 256
HEAVY_LOAD = 72
SEND_PARTS = 4

F32 = jnp.float32
BF16 = jnp.bfloat16
I32 = jnp.int32


class Plan(NamedTuple):
    slots: int
    shift: tuple
    chunk: int
    window: int
    capacity: int
    step: int
    sized: bool

    @property
    def held(self):
        return CHIPS * self.slots

    @property
    def tail(self):
        return -(-self.capacity // WIDTH) * TAIL

    def reach(self, row):
        return row // (self.chunk // self.slots * (self.slots - 1)) * self.chunk

    def block_of(self, lane):
        return (lane * self.shift[0]) >> self.shift[1]

    def slot_of(self, lane):
        return lane - self.slots * self.block_of(lane)

    def first_lane(self):
        return self.slots * (lax.axis_index("yx") * 4 + lax.axis_index("z"))


TIGHT = Plan(24, (2731, 16), 384, 256, 768, 384, True)
ROOMY = Plan(32, (1, 5), 256, 272, 1280, 320, False)


def iota(shape, dim):
    return lax.broadcasted_iota(I32, shape, dim)


def deal(plan, group_hit):
    count = jnp.sum(group_hit, axis=1, keepdims=True)
    count_row = lax.dot_general(
        jnp.ones((8, ROWS), BF16),
        group_hit.astype(BF16),
        (((1,), (1,)), ((), ())),
        preferred_element_type=F32,
    )[:1]
    index = iota((GROUPS, 1), 0)
    index_row = iota((1, GROUPS), 1)
    full = (count == GROUP_CAP).astype(F32)
    heavy = jnp.sum(full * index.astype(F32), axis=0, keepdims=True).astype(I32)
    unsure = jnp.sum(full, axis=0, keepdims=True) != 1.0
    top = jnp.max(jnp.where(index == heavy, 0.0, count), axis=0, keepdims=True)

    def size_class(sizes, where):
        if plan.sized:
            value = (
                (10 * sizes > 7 * top).astype(I32)
                + (20 * sizes > 7 * top).astype(I32)
                + (50 * sizes > 9 * top).astype(I32)
            )
        else:
            value = jnp.zeros(sizes.shape, I32)
        return jnp.where(where == heavy, -1, value)

    mine = size_class(count, index)
    theirs = size_class(count_row, index_row)
    ahead = (theirs > mine) | ((theirs == mine) & (index_row < index))
    order = jnp.sum(ahead.astype(F32), axis=1, keepdims=True).astype(I32)
    coded = jnp.where(mine >= 3, 1.0, 0.0) + jnp.where(mine >= 2, 64.0, 0.0)
    coded = jnp.sum(coded + jnp.where(mine >= 1, 4096.0, 0.0)).astype(I32)
    ends = [coded & 63, (coded >> 6) & 63, coded >> 12]
    loads = [jnp.int32(0), jnp.int32(0), jnp.int32(0), jnp.int32(HEAVY_LOAD)]
    taken = [jnp.int32(0), jnp.int32(0), jnp.int32(0), jnp.int32(1)]
    code = jnp.full((GROUPS, 1), 3 * 32, I32)
    for turn in range(GROUPS - 1):
        if plan.sized:
            weight = jnp.where(
                turn < ends[0], 32, jnp.where(turn < ends[1], 16, jnp.where(turn < ends[2], 8, 4))
            )
        else:
            weight = jnp.int32(14)
        first = loads[1] < loads[0]
        last = loads[3] < loads[2]
        low = jnp.where(first, loads[1], loads[0])
        high = jnp.where(last, loads[3], loads[2])
        kind = jnp.where(high < low, jnp.where(last, 3, 2), jnp.where(first, 1, 0))
        place = taken[0]
        for other in range(1, KINDS):
            place = jnp.where(kind == other, taken[other], place)
        for other in range(KINDS):
            chosen = kind == other
            loads[other] = loads[other] + jnp.where(chosen, weight, 0)
            taken[other] = taken[other] + jnp.where(chosen, 1, 0)
        code = jnp.where(order == turn, kind * 32 + place, code)
    return code, unsure


def send_kernel(plan, ids_ref, rows_ref, out_ref, where_ref, my_ids, my_rows, arrived):
    fetch_ids = pltpu.make_async_copy(ids_ref, my_ids, arrived.at[0])
    fetch_rows = pltpu.make_async_copy(rows_ref, my_rows, arrived.at[1])
    fetch_ids.start()
    fetch_rows.start()
    fetch_ids.wait()
    ids = my_ids[...]
    inner = ids & 15
    hit = iota((GROUPS, ROWS), 0) == (ids >> 4)
    code_of_group, unsure = deal(plan, hit.astype(F32))
    code_of_group = code_of_group.astype(F32)
    code = jnp.sum(jnp.where(hit, code_of_group, 0.0), axis=0, keepdims=True).astype(I32)
    kind, place = code >> 5, code & 31
    odd = (place & 1) == 1
    turned_in_last = (place > 0) & ((place < 4) | odd)
    turned_elsewhere = ((place + 1) & 2) == 2
    in_last = kind == KINDS - 1
    turned = (in_last & turned_in_last) | (~in_last & turned_elsewhere)
    chip = kind * 16 + jnp.where(turned, 15 - inner, inner)

    to_chip = (iota((CHIPS, ROWS), 0) == chip).astype(F32)
    earlier = (iota((ROWS, ROWS), 0) < iota((ROWS, ROWS), 1)).astype(BF16)
    rank = jnp.dot(to_chip.astype(BF16), earlier, preferred_element_type=F32)
    slot = jnp.sum(to_chip * rank, axis=0, keepdims=True).astype(I32)
    over = slot >= plan.slots - 1
    flat = jnp.where(over, -1, chip * plan.slots + slot)
    lane = jnp.where(over, -1, (plan.first_lane() + slot) & (LANES - 1))
    where_ref[...] = jnp.concatenate([chip, lane, jnp.zeros((6, ROWS), I32)], axis=0)
    lost = jnp.max(over.astype(F32), axis=1, keepdims=True)
    flag = jnp.maximum(lost, unsure.astype(F32))

    fetch_rows.wait()
    wide = my_rows[...].astype(F32)
    scale = lax.rsqrt(jnp.sum(wide * wide, axis=1, keepdims=True) + 1e-6)
    normed = (wide * scale).astype(BF16)

    at_lane = (iota((LANES, ROWS), 0) == lane).astype(BF16)
    tagged = (to_chip * (place + 1).astype(F32)).astype(BF16)
    tags = lax.dot_general(tagged, at_lane, (((1,), (1,)), ((), ())), preferred_element_type=F32)
    shown = iota((GROUPS, 128), 1) == iota((GROUPS, 128), 0) + 32
    note = jnp.sum(jnp.where(shown, code_of_group, 0.0), axis=0, keepdims=True)
    note = jnp.where(iota((1, 128), 1) == 0, flag, note)
    meta = jnp.concatenate([tags, jnp.broadcast_to(note, (CHIPS, LANES))], axis=1)
    part = plan.held // SEND_PARTS
    blocks = part // plan.slots
    for first in range(0, plan.held, part):
        row = iota((part, ROWS), 0) + first
        out = jnp.dot((row == flat).astype(BF16), normed, preferred_element_type=F32)
        noted = []
        for block in range(blocks):
            end = (block + 1) * plan.slots
            chip_meta = meta[first // plan.slots + block, :][None, :]
            last = jnp.where(iota((8, 2 * LANES), 0) == 7, chip_meta, 0.0)
            noted.append(out[end - plan.slots : end - 8, : 2 * LANES])
            noted.append(out[end - 8 : end, : 2 * LANES] + last)
        noted = jnp.concatenate(noted, axis=0)
        out = jnp.concatenate([noted, out[:, 2 * LANES :]], axis=1)
        out_ref[pl.ds(first, part), :] = out.astype(BF16)


def compact_kernel(plan, held_ref, out_ref, tags_ref, pos_ref, total_ref, tag_ref):
    held = plan.held
    rows = []
    for source in range(CHIPS):
        at = (source + 1) * plan.slots - 1
        tile = held_ref[pl.ds(at // 16 * 16, 16), : 2 * LANES].astype(F32)
        rows.append(tile[at % 16 : at % 16 + 1])
    meta = jnp.concatenate(rows, axis=0)
    tags = meta[:, :LANES]
    note_top = jnp.max(meta[:, LANES:], axis=0, keepdims=True)
    note_low = jnp.min(meta[:, LANES:], axis=0, keepdims=True)
    note_lane = iota((1, 128), 1)
    flag = jnp.where(note_lane == 0, note_top, 0.0)
    flag = jnp.where(note_lane >= 32, note_top - note_low, flag)
    flag = jnp.max(flag, axis=1, keepdims=True)
    count = jnp.sum((tags > 0).astype(F32), axis=1, keepdims=True)
    before = (iota((CHIPS, CHIPS), 1) < iota((CHIPS, CHIPS), 0)).astype(BF16)
    offset = jnp.dot(
        before, jnp.broadcast_to(count, (CHIPS, 128)).astype(BF16), preferred_element_type=F32
    )[:, :1]
    own_block = plan.block_of(iota((CHIPS, held), 1)) == iota((CHIPS, held), 0)
    tag_row = jnp.sum(
        jnp.where(own_block, jnp.concatenate([tags] * (held // LANES), axis=1), 0.0),
        axis=0,
        keepdims=True,
    )
    offset_row = jnp.sum(jnp.where(own_block, offset, 0.0), axis=0, keepdims=True).astype(I32)
    pos = jnp.where(tag_row > 0, offset_row + plan.slot_of(iota((1, held), 1)), -1)
    pos_ref[...] = jnp.broadcast_to(pos, (8, held))
    per_chunk = plan.chunk // plan.slots
    ahead = iota((CHIPS, LANES), 0) - iota((CHIPS, LANES), 1) * per_chunk
    filled = jnp.where((ahead >= 0) & (ahead < per_chunk), count, 0.0)
    filled = jnp.sum(filled, axis=0, keepdims=True)
    total = jnp.sum(filled, axis=1, keepdims=True)
    over = jnp.max(filled, axis=1, keepdims=True) > plan.window - ALIGN
    over = over | (total > plan.capacity)
    source = iota((CHIPS, 1), 0)
    total_ref[pl.ds(0, ALIGN), :] = jnp.zeros((ALIGN, WIDTH), BF16)
    tag_ref[pl.ds(0, ALIGN), :] = jnp.zeros((ALIGN, LANES), BF16)
    base = 0
    chunk = plan.chunk
    for first in range(0, held, chunk):
        if first:
            low = jnp.sum(jnp.where(source == first // plan.slots, offset, 0.0)).astype(I32)
            base = pl.multiple_of((low >> 4) << 4, ALIGN)
        lanes = slice(first, first + chunk)
        take = (iota((plan.window, chunk), 0) + base) == pos[:, lanes]
        part = jnp.dot(take.astype(BF16), held_ref[lanes, :], preferred_element_type=F32)
        tag = jnp.sum(jnp.where(take, tag_row[:, lanes], 0.0), axis=1, keepdims=True)
        tag = jnp.broadcast_to(tag, (plan.window, LANES)).astype(BF16)
        part = part.astype(BF16)
        head, rest = pl.ds(base, ALIGN), pl.ds(base + ALIGN, plan.window - ALIGN)
        total_ref[head, :] += part[:ALIGN]
        total_ref[rest, :] = part[ALIGN:]
        tag_ref[head, :] += tag[:ALIGN]
        tag_ref[rest, :] = tag[ALIGN:]

    def clear(tile, carry):
        rows = pl.ds(pl.multiple_of(tile * ALIGN, ALIGN), ALIGN)
        total_ref[rows, :] = jnp.zeros((ALIGN, WIDTH), BF16)
        tag_ref[rows, :] = jnp.zeros((ALIGN, LANES), BF16)
        return carry

    lax.fori_loop((base + plan.window) >> 4, plan.capacity // ALIGN, clear, 0)
    out_ref[pl.ds(0, plan.capacity), :] = total_ref[pl.ds(0, plan.capacity), :]
    tags = tag_ref[pl.ds(0, plan.capacity), :]
    tags_ref[...] = tags
    one_lane = (iota((TAIL, LANES), 1) == 0).astype(BF16)
    tag_lanes = lax.dot_general(
        one_lane, tags, (((1,), (1,)), ((), ())), preferred_element_type=F32
    )
    flag = jnp.maximum(flag, over.astype(F32))
    note = jnp.where(note_lane == 0, flag, jnp.where(note_lane >= 32, note_top, 0.0))
    note = jnp.concatenate([note, jnp.zeros((1, plan.capacity - LANES), F32)], axis=1)
    tail = jnp.where(iota((TAIL, plan.capacity), 0) < TAIL // 2, note, tag_lanes)
    for first in range(0, plan.capacity, WIDTH):
        piece = tail[:, first : first + WIDTH].astype(BF16)
        out_ref[pl.ds(plan.capacity + first // WIDTH * TAIL, TAIL), : piece.shape[1]] = piece


def tail_of(plan, ref):
    pieces = []
    for first in range(0, plan.capacity, WIDTH):
        rows = pl.ds(plan.capacity + first // WIDTH * TAIL, TAIL)
        pieces.append(ref[rows, : min(WIDTH, plan.capacity - first)].astype(F32))
    tail = jnp.concatenate(pieces, axis=1)
    return tail[:1, :LANES], tail[TAIL // 2 : TAIL // 2 + 1, :]


def score_block(plan, own_ref, tags_ref, rows_ref, row_tags, start, best, same):
    own = own_ref[pl.ds(start, plan.step), :]
    own_tag = tags_ref[pl.ds(start, plan.step), :1].astype(F32)
    for first in range(0, plan.capacity, COLS):
        rows = rows_ref[pl.ds(first, COLS), :]
        scores = lax.dot_general(
            own, rows, (((1,), (1,)), ((), ())), preferred_element_type=F32
        )
        match = own_tag == row_tags[:, first : first + COLS]
        if same:
            index = iota((plan.step, COLS), 0) + (start - first)
            match = match & (index != iota((plan.step, COLS), 1))
        scores = jnp.where(match, scores, -1.0)
        for lane in range(0, COLS, LANES):
            best = jnp.maximum(best, scores[:, lane : lane + LANES])
    return best


def own_kernel(plan, own_ref, tags_ref, out_ref):
    _, own_tags = tail_of(plan, own_ref)
    for start in range(0, plan.capacity, plan.step):
        best = jnp.full((plan.step, LANES), -1.0, F32)
        best = score_block(plan, own_ref, tags_ref, own_ref, own_tags, start, best, True)
        out_ref[pl.ds(start, plan.step), :] = best


def other_kernel(plan, pos_ref, own_ref, tags_ref, other_ref, part_ref, out_ref):
    own_note, _ = tail_of(plan, own_ref)
    other_note, other_tags = tail_of(plan, other_ref)
    note_lane = iota((1, LANES), 1)
    differs = (note_lane >= 32) & (own_note != other_note)
    raised = jnp.where(note_lane == 0, jnp.maximum(own_note, other_note), 0.0)
    flag = jnp.max(jnp.where(differs, 1.0, raised), axis=1, keepdims=True)
    found = [jnp.zeros((8, plan.chunk), F32)] * (plan.held // plan.chunk)
    for start in range(0, plan.capacity, plan.step):
        best = part_ref[pl.ds(start, plan.step), :]
        best = score_block(plan, own_ref, tags_ref, other_ref, other_tags, start, best, False)
        top = jnp.max(best, axis=1, keepdims=True)
        row = iota((plan.step, plan.chunk), 0) + start
        for index in range(plan.reach(start) // plan.chunk, plan.held // plan.chunk):
            pos = pos_ref[0:1, index * plan.chunk : (index + 1) * plan.chunk]
            value = jnp.where(row == pos, top, 0.0)
            found[index] += jnp.sum(value.reshape(plan.step // 8, 8, plan.chunk), axis=0)

    blocks = plan.chunk // plan.slots
    for index, values in enumerate(found):
        lane = iota((1, plan.chunk), 1)
        values = jnp.sum(values, axis=0, keepdims=True)
        values = jnp.where(plan.slot_of(lane) == plan.slots - 1, flag, values)
        in_block = plan.block_of(lane) == iota((blocks, plan.chunk), 0)
        mine = jnp.where(in_block, values, 0.0)
        folded = mine[:, :LANES]
        for first in range(LANES, plan.chunk, LANES):
            folded = folded + mine[:, first : first + LANES]
        out_ref[index * blocks : (index + 1) * blocks, :] = folded


def answer_kernel(plan, where_ref, back_ref, out_ref, flag_ref):
    chip = where_ref[0:1, :]
    lane = where_ref[1:2, :]
    back = back_ref[...]
    to_chip = (iota((CHIPS, ROWS), 0) == chip).astype(BF16)
    high = back.astype(BF16)
    rest = back - high.astype(F32)
    middle = rest.astype(BF16)
    low = (rest - middle.astype(F32)).astype(BF16)
    parts = jnp.concatenate([high, middle, low], axis=1)
    by_row = lax.dot_general(
        parts, to_chip, (((0,), (0,)), ((), ())), preferred_element_type=F32
    )
    by_row = (by_row[:LANES] + by_row[LANES : 2 * LANES]) + by_row[2 * LANES :]
    at_lane = iota((LANES, ROWS), 0) == lane
    out_ref[...] = jnp.sum(jnp.where(at_lane, by_row, 0.0), axis=0, keepdims=True)
    last = iota((CHIPS, LANES), 1) == ((plan.first_lane() + plan.slots - 1) & (LANES - 1))
    flag_ref[0] = (jnp.max(jnp.where(last, back, 0.0)) > 0.0).astype(I32)


VMEM = pl.BlockSpec(memory_space=pltpu.VMEM)
SMEM = pl.BlockSpec(memory_space=pltpu.SMEM)
HBM = pl.BlockSpec(memory_space=pltpu.HBM)


def shape(dims, dtype):
    return jax.ShapeDtypeStruct(dims, dtype)


def call(kernel, plan, name, **options):
    return pl.pallas_call(
        functools.partial(kernel, plan),
        compiler_params=pltpu.CompilerParams(vmem_limit_bytes=48 * 1024 * 1024),
        name=name,
        **options,
    )


def swap(plan, message):
    return lax.all_to_all(message, ("yx", "z"), split_axis=0, concat_axis=0, tiled=True)


def owner_path(plan, embeddings, cluster_ids):
    message, where = call(
        send_kernel,
        plan,
        "send",
        out_shape=(shape((plan.held, WIDTH), BF16), shape((8, ROWS), I32)),
        in_specs=[HBM, HBM],
        out_specs=(VMEM, VMEM),
        scratch_shapes=[
            pltpu.VMEM((1, ROWS), I32),
            pltpu.VMEM((ROWS, WIDTH), BF16),
            pltpu.SemaphoreType.DMA((2,)),
        ],
    )(cluster_ids.reshape(1, ROWS), embeddings)
    held = swap(plan, message)
    packed, tags, pos = call(
        compact_kernel,
        plan,
        "compact",
        out_shape=(
            shape((plan.capacity + plan.tail, WIDTH), BF16),
            shape((plan.capacity, LANES), BF16),
            shape((8, plan.held), I32),
        ),
        in_specs=[VMEM],
        out_specs=(VMEM, VMEM, VMEM),
        scratch_shapes=[
            pltpu.VMEM((plan.held + plan.window, WIDTH), BF16),
            pltpu.VMEM((plan.held + plan.window, LANES), BF16),
        ],
    )(held)
    other = lax.ppermute(packed, "core", [(0, 1), (1, 0)])
    part = call(
        own_kernel,
        plan,
        "score_own",
        out_shape=shape((plan.capacity, LANES), F32),
        in_specs=[VMEM, VMEM],
        out_specs=VMEM,
        cost_estimate=pl.CostEstimate(
            flops=2 * plan.capacity**2 * WIDTH,
            bytes_accessed=2 * plan.capacity * WIDTH,
            transcendentals=0,
        ),
    )(packed, tags)
    best = call(
        other_kernel,
        plan,
        "score_other",
        out_shape=shape((CHIPS, LANES), F32),
        in_specs=[VMEM] * 5,
        out_specs=VMEM,
    )(pos, packed, tags, other, part)
    back = swap(plan, best)
    answer, flag = call(
        answer_kernel,
        plan,
        "answer",
        out_shape=(shape((1, ROWS), F32), shape((1,), I32)),
        in_specs=[VMEM, VMEM],
        out_specs=(VMEM, SMEM),
    )(where, back)
    return answer.reshape(ROWS), flag[0]


def pair_max(left_rows, left_ids, left_pos, right_rows, right_ids, right_pos):
    left_total, width = left_rows.shape
    left_step = min(512, left_total)
    left_count = left_total // left_step

    def left_turn(carry, left_tuple):
        part_rows, part_ids, part_pos = left_tuple
        scores = lax.dot_general(
            part_rows, right_rows, (((1,), (1,)), ((), ())), preferred_element_type=F32
        )
        matches = (
            (part_ids[:, None] == right_ids[None, :])
            & (part_ids[:, None] >= 0)
            & (part_pos[:, None] != right_pos[None, :])
        )
        return carry, jnp.max(jnp.where(matches, scores, -1.0), axis=1)

    _, row_best = lax.scan(
        left_turn,
        0,
        (
            left_rows.reshape(left_count, left_step, width),
            left_ids.reshape(left_count, left_step),
            left_pos.reshape(left_count, left_step),
        ),
    )
    return row_best.reshape(-1)


def gather(piece):
    copies = jnp.broadcast_to(piece[None], (4, *piece.shape))
    whole = lax.all_to_all(copies, "z", split_axis=0, concat_axis=0, tiled=True)
    return whole.reshape(-1, *piece.shape[1:])


def any_path(embeddings, cluster_ids):
    axes = ("yx", "core")
    widened = embeddings.astype(F32)
    normed = (
        widened * lax.rsqrt(jnp.sum(widened * widened, axis=1, keepdims=True) + 1e-06)
    ).astype(BF16)
    owner_group = cluster_ids // CL_GRP
    one_hot = (owner_group[:, None] == jnp.arange(GROUPS, dtype=I32)[None, :]).astype(I32)
    slot_index = jnp.sum(jnp.cumsum(one_hot, axis=0) * one_hot, axis=1) - 1
    flat_slot = owner_group * GROUP_CAP + slot_index
    total = GROUPS * GROUP_CAP
    placement = jnp.arange(total, dtype=I32)[:, None] == flat_slot[None, :]
    outgoing = jnp.dot(placement.astype(BF16), normed, preferred_element_type=F32).astype(BF16)
    outgoing = outgoing.reshape(GROUPS, GROUP_CAP, WIDTH)
    outgoing_ids = jnp.max(jnp.where(placement, cluster_ids[None, :], -1), axis=1)
    outgoing_ids = outgoing_ids.reshape(GROUPS, GROUP_CAP)
    received = lax.all_to_all(outgoing, axes, 0, 0, tiled=True).reshape(total, WIDTH)
    received_ids = lax.all_to_all(outgoing_ids, axes, 0, 0, tiled=True).reshape(total)
    own_pos = jnp.arange(total, dtype=I32) + lax.axis_index("z") * total
    piece_rows = gather(received)
    piece_ids = gather(received_ids)
    piece_pos = jnp.arange(piece_rows.shape[0], dtype=I32)
    best = pair_max(received, received_ids, own_pos, piece_rows, piece_ids, piece_pos)
    best = jnp.maximum(best, -1.0)
    returned = lax.all_to_all(best.reshape(GROUPS, GROUP_CAP), axes, 0, 0, tiled=True)
    return jnp.max(jnp.where(placement, returned.reshape(total)[:, None], -2.0), axis=0)


def body(embeddings, cluster_ids):
    def keep(rows, ids, done):
        return done

    def last_resort(rows, ids, done):
        return any_path(rows, ids)

    def roomy(rows, ids, done):
        answer, flag = owner_path(ROOMY, rows, ids)
        return lax.switch(flag, [keep, last_resort], rows, ids, answer)

    answer, flag = owner_path(TIGHT, embeddings, cluster_ids)
    embeddings, cluster_ids, answer, flag = lax.optimization_barrier(
        (embeddings, cluster_ids, answer, flag)
    )
    return lax.switch(flag, [keep, roomy], embeddings, cluster_ids, answer)


def solution(mesh):
    chips = Mesh(np.asarray(mesh.devices).reshape(16, 2, 4), ("yx", "core", "z"))
    axes = ("yx", "core", "z")
    return jax.shard_map(
        body, mesh=chips, in_specs=(P(axes, None), P(axes)), out_specs=P(axes), check_vma=False
    )
```

```python
import functools
from typing import NamedTuple

import jax
import jax.numpy as jnp
import numpy as np
from jax import lax
from jax.experimental import pallas as pl
from jax.experimental.pallas import tpu as pltpu
from jax.sharding import Mesh
from jax.sharding import PartitionSpec as P

CL_GRP = 16
GROUPS = 32
GROUP_CAP = 64
WIDTH = 768
ROWS = 512
CHIPS = 64
KINDS = 4
TAIL = 16
LANES = 128
ALIGN = 16
COLS = 256
HEAVY_LOAD = 72
SEND_PARTS = 4

F32 = jnp.float32
BF16 = jnp.bfloat16
I32 = jnp.int32


class Plan(NamedTuple):
    slots: int
    shift: tuple
    chunk: int
    window: int
    capacity: int
    step: int
    sized: bool

    @property
    def held(self):
        return CHIPS * self.slots

    @property
    def tail(self):
        return -(-self.capacity // WIDTH) * TAIL

    def reach(self, row):
        return row // (self.chunk // self.slots * (self.slots - 1)) * self.chunk

    def block_of(self, lane):
        return (lane * self.shift[0]) >> self.shift[1]

    def slot_of(self, lane):
        return lane - self.slots * self.block_of(lane)

    def first_lane(self):
        return self.slots * (lax.axis_index("yx") * 4 + lax.axis_index("z"))


TIGHT = Plan(24, (2731, 16), 384, 256, 768, 384, True)
ROOMY = Plan(32, (1, 5), 256, 272, 1280, 320, False)


def iota(shape, dim):
    return lax.broadcasted_iota(I32, shape, dim)


def deal(plan, group_hit, meanwhile):
    count = jnp.sum(group_hit, axis=1, keepdims=True)
    count_row = lax.dot_general(
        jnp.ones((8, ROWS), BF16),
        group_hit.astype(BF16),
        (((1,), (1,)), ((), ())),
        preferred_element_type=F32,
    )[:1]
    index = iota((GROUPS, 1), 0)
    index_row = iota((1, GROUPS), 1)
    full = (count == GROUP_CAP).astype(F32)
    heavy = jnp.sum(full * index.astype(F32), axis=0, keepdims=True).astype(I32)
    unsure = jnp.sum(full, axis=0, keepdims=True) != 1.0
    top = jnp.max(jnp.where(index == heavy, 0.0, count), axis=0, keepdims=True)

    def size_class(sizes, where):
        if plan.sized:
            value = (
                (10 * sizes > 7 * top).astype(I32)
                + (20 * sizes > 7 * top).astype(I32)
                + (50 * sizes > 9 * top).astype(I32)
            )
        else:
            value = jnp.zeros(sizes.shape, I32)
        return jnp.where(where == heavy, -1, value)

    mine = size_class(count, index)
    theirs = size_class(count_row, index_row)
    ahead = (theirs > mine) | ((theirs == mine) & (index_row < index))
    order = jnp.sum(ahead.astype(F32), axis=1, keepdims=True).astype(I32)
    coded = jnp.where(mine >= 3, 1.0, 0.0) + jnp.where(mine >= 2, 64.0, 0.0)
    coded = jnp.sum(coded + jnp.where(mine >= 1, 4096.0, 0.0)).astype(I32)
    ends = [coded & 63, (coded >> 6) & 63, coded >> 12]
    other_work = meanwhile()
    loads = [jnp.int32(0), jnp.int32(0), jnp.int32(0), jnp.int32(HEAVY_LOAD)]
    taken = [jnp.int32(0), jnp.int32(0), jnp.int32(0), jnp.int32(1)]
    code = jnp.full((GROUPS, 1), 3 * 32, I32)
    for turn in range(GROUPS - 1):
        if plan.sized:
            weight = jnp.where(
                turn < ends[0], 32, jnp.where(turn < ends[1], 16, jnp.where(turn < ends[2], 8, 4))
            )
        else:
            weight = jnp.int32(14)
        first = loads[1] < loads[0]
        last = loads[3] < loads[2]
        low = jnp.where(first, loads[1], loads[0])
        high = jnp.where(last, loads[3], loads[2])
        kind = jnp.where(high < low, jnp.where(last, 3, 2), jnp.where(first, 1, 0))
        place = taken[0]
        for other in range(1, KINDS):
            place = jnp.where(kind == other, taken[other], place)
        for other in range(KINDS):
            chosen = kind == other
            loads[other] = loads[other] + jnp.where(chosen, weight, 0)
            taken[other] = taken[other] + jnp.where(chosen, 1, 0)
        code = jnp.where(order == turn, kind * 32 + place, code)
    return code, unsure, other_work


def send_kernel(plan, ids_ref, rows_ref, out_ref, where_ref, my_ids, my_rows, arrived):
    fetch_ids = pltpu.make_async_copy(ids_ref, my_ids, arrived.at[0])
    fetch_rows = pltpu.make_async_copy(rows_ref, my_rows, arrived.at[1])
    fetch_ids.start()
    fetch_rows.start()
    fetch_ids.wait()
    ids = my_ids[...]
    inner = ids & 15
    hit = iota((GROUPS, ROWS), 0) == (ids >> 4)

    def normalise():
        fetch_rows.wait()
        wide = my_rows[...].astype(F32)
        scale = lax.rsqrt(jnp.sum(wide * wide, axis=1, keepdims=True) + 1e-6)
        return (wide * scale).astype(BF16)

    code_of_group, unsure, normed = deal(plan, hit.astype(F32), normalise)
    code_of_group = code_of_group.astype(F32)
    code = jnp.sum(jnp.where(hit, code_of_group, 0.0), axis=0, keepdims=True).astype(I32)
    kind, place = code >> 5, code & 31
    odd = (place & 1) == 1
    turned_in_last = (place > 0) & ((place < 4) | odd)
    turned_elsewhere = ((place + 1) & 2) == 2
    in_last = kind == KINDS - 1
    turned = (in_last & turned_in_last) | (~in_last & turned_elsewhere)
    chip = kind * 16 + jnp.where(turned, 15 - inner, inner)

    to_chip = (iota((CHIPS, ROWS), 0) == chip).astype(F32)
    earlier = (iota((ROWS, ROWS), 0) < iota((ROWS, ROWS), 1)).astype(BF16)
    rank = jnp.dot(to_chip.astype(BF16), earlier, preferred_element_type=F32)
    slot = jnp.sum(to_chip * rank, axis=0, keepdims=True).astype(I32)
    over = slot >= plan.slots - 1
    flat = jnp.where(over, -1, chip * plan.slots + slot)
    lane = jnp.where(over, -1, (plan.first_lane() + slot) & (LANES - 1))
    where_ref[...] = jnp.concatenate([chip, lane, jnp.zeros((6, ROWS), I32)], axis=0)
    lost = jnp.max(over.astype(F32), axis=1, keepdims=True)
    flag = jnp.maximum(lost, unsure.astype(F32))

    at_lane = (iota((LANES, ROWS), 0) == lane).astype(BF16)
    tagged = (to_chip * (place + 1).astype(F32)).astype(BF16)
    tags = lax.dot_general(tagged, at_lane, (((1,), (1,)), ((), ())), preferred_element_type=F32)
    shown = iota((GROUPS, 128), 1) == iota((GROUPS, 128), 0) + 32
    note = jnp.sum(jnp.where(shown, code_of_group, 0.0), axis=0, keepdims=True)
    sent = jnp.sum(to_chip, axis=1, keepdims=True)
    shown = iota((CHIPS, LANES), 1) == iota((CHIPS, LANES), 0) + 64
    note += jnp.sum(jnp.where(shown, sent, 0.0), axis=0, keepdims=True)
    note = jnp.where(iota((1, LANES), 1) == 0, flag, note)
    meta = jnp.concatenate([tags, jnp.broadcast_to(note, (CHIPS, LANES))], axis=1)
    part = plan.held // SEND_PARTS
    blocks = part // plan.slots
    for first in range(0, plan.held, part):
        row = iota((part, ROWS), 0) + first
        out = jnp.dot((row == flat).astype(BF16), normed, preferred_element_type=F32)
        noted = []
        for block in range(blocks):
            end = (block + 1) * plan.slots
            chip_meta = meta[first // plan.slots + block, :][None, :]
            last = jnp.where(iota((8, 2 * LANES), 0) == 7, chip_meta, 0.0)
            noted.append(out[end - plan.slots : end - 8, : 2 * LANES])
            noted.append(out[end - 8 : end, : 2 * LANES] + last)
        noted = jnp.concatenate(noted, axis=0)
        out = jnp.concatenate([noted, out[:, 2 * LANES :]], axis=1)
        out_ref[pl.ds(first, part), :] = out.astype(BF16)


def compact_kernel(plan, held_ref, out_ref, tags_ref, pos_ref, note_ref, total_ref, tag_ref):
    held = plan.held
    rows = []
    for source in range(CHIPS):
        at = (source + 1) * plan.slots - 1
        tile = held_ref[pl.ds(at // 16 * 16, 16), : 2 * LANES].astype(F32)
        rows.append(tile[at % 16 : at % 16 + 1])
    meta = jnp.concatenate(rows, axis=0)
    tags = meta[:, :LANES]
    note_top = jnp.max(meta[:, LANES:], axis=0, keepdims=True)
    note_low = jnp.min(meta[:, LANES:], axis=0, keepdims=True)
    note_lane = iota((1, LANES), 1)
    per_chunk = plan.chunk // plan.slots
    filled = jnp.sum(meta[:, LANES:].reshape(CHIPS // per_chunk, per_chunk, LANES), axis=1)
    total = jnp.sum(filled, axis=0, keepdims=True)
    filled = jnp.max(filled, axis=0, keepdims=True)
    over = (filled > plan.window - ALIGN) | (total > plan.capacity)
    flag = jnp.where(note_lane == 0, note_top, 0.0)
    flag = jnp.where((note_lane >= 32) & (note_lane < 64), note_top - note_low, flag)
    flag = jnp.where(note_lane >= 64, over.astype(F32), flag)
    flag = jnp.max(flag, axis=1, keepdims=True)
    note = jnp.where(note_lane == 0, flag, jnp.where(note_lane < 64, note_top, 0.0))
    note_ref[...] = jnp.broadcast_to(note, (8, LANES))
    count = jnp.sum((tags > 0).astype(F32), axis=1, keepdims=True)
    before = (iota((CHIPS, CHIPS), 1) < iota((CHIPS, CHIPS), 0)).astype(BF16)
    offset = jnp.dot(
        before, jnp.broadcast_to(count, (CHIPS, 128)).astype(BF16), preferred_element_type=F32
    )[:, :1]
    own_block = plan.block_of(iota((CHIPS, held), 1)) == iota((CHIPS, held), 0)
    tag_row = jnp.sum(
        jnp.where(own_block, jnp.concatenate([tags] * (held // LANES), axis=1), 0.0),
        axis=0,
        keepdims=True,
    )
    offset_row = jnp.sum(jnp.where(own_block, offset, 0.0), axis=0, keepdims=True).astype(I32)
    pos = jnp.where(tag_row > 0, offset_row + plan.slot_of(iota((1, held), 1)), -1)
    pos_ref[...] = jnp.broadcast_to(pos, (8, held))
    source = iota((CHIPS, 1), 0)
    total_ref[pl.ds(0, ALIGN), :] = jnp.zeros((ALIGN, WIDTH), BF16)
    tag_ref[pl.ds(0, ALIGN), :] = jnp.zeros((ALIGN, LANES), BF16)
    base = 0
    chunk = plan.chunk
    for first in range(0, held, chunk):
        if first:
            low = jnp.sum(jnp.where(source == first // plan.slots, offset, 0.0)).astype(I32)
            base = pl.multiple_of((low >> 4) << 4, ALIGN)
        lanes = slice(first, first + chunk)
        take = (iota((plan.window, chunk), 0) + base) == pos[:, lanes]
        part = jnp.dot(take.astype(BF16), held_ref[lanes, :], preferred_element_type=F32)
        tag = jnp.sum(jnp.where(take, tag_row[:, lanes], 0.0), axis=1, keepdims=True)
        tag = jnp.broadcast_to(tag, (plan.window, LANES)).astype(BF16)
        part = part.astype(BF16)
        head, rest = pl.ds(base, ALIGN), pl.ds(base + ALIGN, plan.window - ALIGN)
        total_ref[head, :] += part[:ALIGN]
        total_ref[rest, :] = part[ALIGN:]
        tag_ref[head, :] += tag[:ALIGN]
        tag_ref[rest, :] = tag[ALIGN:]

    def clear(tile, carry):
        rows = pl.ds(pl.multiple_of(tile * ALIGN, ALIGN), ALIGN)
        total_ref[rows, :] = jnp.zeros((ALIGN, WIDTH), BF16)
        tag_ref[rows, :] = jnp.zeros((ALIGN, LANES), BF16)
        return carry

    lax.fori_loop((base + plan.window) >> 4, plan.capacity // ALIGN, clear, 0)
    out_ref[pl.ds(0, plan.capacity), :] = total_ref[pl.ds(0, plan.capacity), :]
    tags = tag_ref[pl.ds(0, plan.capacity), :]
    tags_ref[...] = tags
    one_lane = (iota((TAIL, LANES), 1) == 0).astype(BF16)
    tag_lanes = lax.dot_general(
        one_lane, tags, (((1,), (1,)), ((), ())), preferred_element_type=F32
    )
    for first in range(0, plan.capacity, WIDTH):
        piece = tag_lanes[:, first : first + WIDTH].astype(BF16)
        out_ref[pl.ds(plan.capacity + first // WIDTH * TAIL, TAIL), : piece.shape[1]] = piece


def row_tags(plan, ref):
    pieces = []
    for first in range(0, plan.capacity, WIDTH):
        rows = pl.ds(plan.capacity + first // WIDTH * TAIL, TAIL)
        pieces.append(ref[rows, : min(WIDTH, plan.capacity - first)].astype(F32))
    return jnp.concatenate(pieces, axis=1)[:1]


def flag_kernel(plan, own_ref, other_ref, flag_ref):
    own, other = own_ref[...], other_ref[...]
    lane = iota((8, LANES), 1)
    raised = jnp.where(lane == 0, jnp.maximum(own, other), 0.0)
    raised = jnp.where((lane >= 32) & (own != other), 1.0, raised)
    flag_ref[0] = (jnp.max(raised) > 0.0).astype(I32)


def score_block(plan, own_ref, tags_ref, rows_ref, their_tags, start, best, same):
    own = own_ref[pl.ds(start, plan.step), :]
    own_tag = tags_ref[pl.ds(start, plan.step), :1].astype(F32)
    for first in range(0, plan.capacity, COLS):
        rows = rows_ref[pl.ds(first, COLS), :]
        scores = lax.dot_general(
            own, rows, (((1,), (1,)), ((), ())), preferred_element_type=F32
        )
        match = own_tag == their_tags[:, first : first + COLS]
        if same:
            index = iota((plan.step, COLS), 0) + (start - first)
            match = match & (index != iota((plan.step, COLS), 1))
        scores = jnp.where(match, scores, -1.0)
        for lane in range(0, COLS, LANES):
            best = jnp.maximum(best, scores[:, lane : lane + LANES])
    return best


def own_kernel(plan, own_ref, tags_ref, out_ref):
    own_tags = row_tags(plan, own_ref)
    for start in range(0, plan.capacity, plan.step):
        best = jnp.full((plan.step, LANES), -1.0, F32)
        best = score_block(plan, own_ref, tags_ref, own_ref, own_tags, start, best, True)
        out_ref[pl.ds(start, plan.step), :] = best


def other_kernel(plan, pos_ref, own_ref, tags_ref, other_ref, part_ref, _, out_ref):
    other_tags = row_tags(plan, other_ref)
    found = [jnp.zeros((8, plan.chunk), F32)] * (plan.held // plan.chunk)
    for start in range(0, plan.capacity, plan.step):
        best = part_ref[pl.ds(start, plan.step), :]
        best = score_block(plan, own_ref, tags_ref, other_ref, other_tags, start, best, False)
        top = jnp.max(best, axis=1, keepdims=True)
        row = iota((plan.step, plan.chunk), 0) + start
        for index in range(plan.reach(start) // plan.chunk, plan.held // plan.chunk):
            pos = pos_ref[0:1, index * plan.chunk : (index + 1) * plan.chunk]
            value = jnp.where(row == pos, top, 0.0)
            found[index] += jnp.sum(value.reshape(plan.step // 8, 8, plan.chunk), axis=0)

    blocks = plan.chunk // plan.slots
    for index, values in enumerate(found):
        lane = iota((1, plan.chunk), 1)
        values = jnp.sum(values, axis=0, keepdims=True)
        in_block = plan.block_of(lane) == iota((blocks, plan.chunk), 0)
        mine = jnp.where(in_block, values, 0.0)
        folded = mine[:, :LANES]
        for first in range(LANES, plan.chunk, LANES):
            folded = folded + mine[:, first : first + LANES]
        out_ref[index * blocks : (index + 1) * blocks, :] = folded


def answer_kernel(plan, where_ref, back_ref, out_ref):
    chip = where_ref[0:1, :]
    lane = where_ref[1:2, :]
    back = back_ref[...]
    to_chip = (iota((CHIPS, ROWS), 0) == chip).astype(BF16)
    high = back.astype(BF16)
    rest = back - high.astype(F32)
    middle = rest.astype(BF16)
    low = (rest - middle.astype(F32)).astype(BF16)
    parts = jnp.concatenate([high, middle, low], axis=1)
    by_row = lax.dot_general(
        parts, to_chip, (((0,), (0,)), ((), ())), preferred_element_type=F32
    )
    by_row = (by_row[:LANES] + by_row[LANES : 2 * LANES]) + by_row[2 * LANES :]
    at_lane = iota((LANES, ROWS), 0) == lane
    out_ref[...] = jnp.sum(jnp.where(at_lane, by_row, 0.0), axis=0, keepdims=True)


VMEM = pl.BlockSpec(memory_space=pltpu.VMEM)
SMEM = pl.BlockSpec(memory_space=pltpu.SMEM)
HBM = pl.BlockSpec(memory_space=pltpu.HBM)


def shape(dims, dtype):
    return jax.ShapeDtypeStruct(dims, dtype)


def call(kernel, plan, name, **options):
    return pl.pallas_call(
        functools.partial(kernel, plan),
        compiler_params=pltpu.CompilerParams(vmem_limit_bytes=48 * 1024 * 1024),
        name=name,
        **options,
    )


def swap(plan, message):
    return lax.all_to_all(message, ("yx", "z"), split_axis=0, concat_axis=0, tiled=True)


def owner_path(plan, embeddings, cluster_ids):
    message, where = call(
        send_kernel,
        plan,
        "send",
        out_shape=(shape((plan.held, WIDTH), BF16), shape((8, ROWS), I32)),
        in_specs=[HBM, HBM],
        out_specs=(VMEM, VMEM),
        scratch_shapes=[
            pltpu.VMEM((1, ROWS), I32),
            pltpu.VMEM((ROWS, WIDTH), BF16),
            pltpu.SemaphoreType.DMA((2,)),
        ],
    )(cluster_ids.reshape(1, ROWS), embeddings)
    held = swap(plan, message)
    packed, tags, pos, note = call(
        compact_kernel,
        plan,
        "compact",
        out_shape=(
            shape((plan.capacity + plan.tail, WIDTH), BF16),
            shape((plan.capacity, LANES), BF16),
            shape((8, plan.held), I32),
            shape((8, LANES), F32),
        ),
        in_specs=[VMEM],
        out_specs=(VMEM,) * 4,
        scratch_shapes=[
            pltpu.VMEM((plan.held + plan.window, WIDTH), BF16),
            pltpu.VMEM((plan.held + plan.window, LANES), BF16),
        ],
    )(held)
    pairs = [(0, 1), (1, 0)]
    other_note = lax.ppermute(note, "core", pairs)
    other = lax.ppermute(packed, "core", pairs)
    part = call(
        own_kernel,
        plan,
        "score_own",
        out_shape=shape((plan.capacity, LANES), F32),
        in_specs=[VMEM, VMEM],
        out_specs=VMEM,
        cost_estimate=pl.CostEstimate(
            flops=2 * plan.capacity**2 * WIDTH,
            bytes_accessed=2 * plan.capacity * WIDTH,
            transcendentals=0,
        ),
    )(packed, tags)
    flag = call(
        flag_kernel,
        plan,
        "flag",
        out_shape=shape((1,), I32),
        in_specs=[VMEM, VMEM],
        out_specs=SMEM,
    )(note, other_note)
    flag = lax.clamp(0, flag[0], 1)
    best = call(
        other_kernel,
        plan,
        "score_other",
        out_shape=shape((CHIPS, LANES), F32),
        in_specs=[VMEM] * 5 + [pl.BlockSpec(memory_space=pl.ANY)],
        out_specs=VMEM,
    )(pos, packed, tags, other, part, flag.reshape(1))
    back = swap(plan, best)
    answer = call(
        answer_kernel,
        plan,
        "answer",
        out_shape=shape((1, ROWS), F32),
        in_specs=[VMEM] * 2,
        out_specs=VMEM,
    )(where, back)
    return answer.reshape(ROWS), flag


def pair_max(left_rows, left_ids, left_pos, right_rows, right_ids, right_pos):
    left_total, width = left_rows.shape
    left_step = min(512, left_total)
    left_count = left_total // left_step

    def left_turn(carry, left_tuple):
        part_rows, part_ids, part_pos = left_tuple
        scores = lax.dot_general(
            part_rows, right_rows, (((1,), (1,)), ((), ())), preferred_element_type=F32
        )
        matches = (
            (part_ids[:, None] == right_ids[None, :])
            & (part_ids[:, None] >= 0)
            & (part_pos[:, None] != right_pos[None, :])
        )
        return carry, jnp.max(jnp.where(matches, scores, -1.0), axis=1)

    _, row_best = lax.scan(
        left_turn,
        0,
        (
            left_rows.reshape(left_count, left_step, width),
            left_ids.reshape(left_count, left_step),
            left_pos.reshape(left_count, left_step),
        ),
    )
    return row_best.reshape(-1)


def gather(piece):
    copies = jnp.broadcast_to(piece[None], (4, *piece.shape))
    whole = lax.all_to_all(copies, "z", split_axis=0, concat_axis=0, tiled=True)
    return whole.reshape(-1, *piece.shape[1:])


def any_path(embeddings, cluster_ids):
    axes = ("yx", "core")
    widened = embeddings.astype(F32)
    normed = (
        widened * lax.rsqrt(jnp.sum(widened * widened, axis=1, keepdims=True) + 1e-06)
    ).astype(BF16)
    owner_group = cluster_ids // CL_GRP
    one_hot = (owner_group[:, None] == jnp.arange(GROUPS, dtype=I32)[None, :]).astype(I32)
    slot_index = jnp.sum(jnp.cumsum(one_hot, axis=0) * one_hot, axis=1) - 1
    flat_slot = owner_group * GROUP_CAP + slot_index
    total = GROUPS * GROUP_CAP
    placement = jnp.arange(total, dtype=I32)[:, None] == flat_slot[None, :]
    outgoing = jnp.dot(placement.astype(BF16), normed, preferred_element_type=F32).astype(BF16)
    outgoing = outgoing.reshape(GROUPS, GROUP_CAP, WIDTH)
    outgoing_ids = jnp.max(jnp.where(placement, cluster_ids[None, :], -1), axis=1)
    outgoing_ids = outgoing_ids.reshape(GROUPS, GROUP_CAP)
    received = lax.all_to_all(outgoing, axes, 0, 0, tiled=True).reshape(total, WIDTH)
    received_ids = lax.all_to_all(outgoing_ids, axes, 0, 0, tiled=True).reshape(total)
    own_pos = jnp.arange(total, dtype=I32) + lax.axis_index("z") * total
    piece_rows = gather(received)
    piece_ids = gather(received_ids)
    piece_pos = jnp.arange(piece_rows.shape[0], dtype=I32)
    best = pair_max(received, received_ids, own_pos, piece_rows, piece_ids, piece_pos)
    best = jnp.maximum(best, -1.0)
    returned = lax.all_to_all(best.reshape(GROUPS, GROUP_CAP), axes, 0, 0, tiled=True)
    return jnp.max(jnp.where(placement, returned.reshape(total)[:, None], -2.0), axis=0)


def body(embeddings, cluster_ids):
    def keep(rows, ids, done):
        return done

    def last_resort(rows, ids, done):
        return any_path(rows, ids)

    def roomy(rows, ids, done):
        answer, flag = owner_path(ROOMY, rows, ids)
        return lax.switch(flag, [keep, last_resort], rows, ids, answer)

    answer, flag = owner_path(TIGHT, embeddings, cluster_ids)
    embeddings, cluster_ids, answer = lax.optimization_barrier(
        (embeddings, cluster_ids, answer)
    )
    return lax.switch(flag, [keep, roomy], embeddings, cluster_ids, answer)


def solution(mesh):
    chips = Mesh(np.asarray(mesh.devices).reshape(16, 2, 4), ("yx", "core", "z"))
    axes = ("yx", "core", "z")
    return jax.shard_map(
        body, mesh=chips, in_specs=(P(axes, None), P(axes)), out_specs=P(axes), check_vma=False
    )
```

```python
import functools
from typing import NamedTuple

import jax
import jax.numpy as jnp
import numpy as np
from jax import lax
from jax.experimental import pallas as pl
from jax.experimental.pallas import tpu as pltpu
from jax.sharding import Mesh
from jax.sharding import PartitionSpec as P

CL_GRP = 16
GROUPS = 32
GROUP_CAP = 64
WIDTH = 768
ROWS = 512
CHIPS = 64
KINDS = 4
TAIL = 16
LANES = 128
ALIGN = 16
COLS = 256
HEAVY_LOAD = 72
SEND_PARTS = 4

F32 = jnp.float32
BF16 = jnp.bfloat16
I32 = jnp.int32


class Plan(NamedTuple):
    slots: int
    shift: tuple
    chunk: int
    window: int
    capacity: int
    step: int
    sized: bool

    @property
    def held(self):
        return CHIPS * self.slots

    @property
    def tail(self):
        return -(-self.capacity // WIDTH) * TAIL

    def reach(self, row):
        return row // (self.chunk // self.slots * (self.slots - 1)) * self.chunk

    def block_of(self, lane):
        return (lane * self.shift[0]) >> self.shift[1]

    def slot_of(self, lane):
        return lane - self.slots * self.block_of(lane)

    def first_lane(self):
        return self.slots * (lax.axis_index("yx") * 4 + lax.axis_index("z"))


TIGHT = Plan(24, (2731, 16), 384, 256, 768, 384, True)
ROOMY = Plan(32, (1, 5), 256, 272, 1280, 320, False)


def iota(shape, dim):
    return lax.broadcasted_iota(I32, shape, dim)


def deal(plan, group_hit):
    count = jnp.sum(group_hit, axis=1, keepdims=True)
    count_row = lax.dot_general(
        jnp.ones((8, ROWS), BF16),
        group_hit.astype(BF16),
        (((1,), (1,)), ((), ())),
        preferred_element_type=F32,
    )[:1]
    index = iota((GROUPS, 1), 0)
    index_row = iota((1, GROUPS), 1)
    full = (count == GROUP_CAP).astype(F32)
    heavy = jnp.sum(full * index.astype(F32), axis=0, keepdims=True).astype(I32)
    unsure = jnp.sum(full, axis=0, keepdims=True) != 1.0
    top = jnp.max(jnp.where(index == heavy, 0.0, count), axis=0, keepdims=True)

    def size_class(sizes, where):
        if plan.sized:
            value = (
                (10 * sizes > 7 * top).astype(I32)
                + (20 * sizes > 7 * top).astype(I32)
                + (50 * sizes > 9 * top).astype(I32)
            )
        else:
            value = jnp.zeros(sizes.shape, I32)
        return jnp.where(where == heavy, -1, value)

    mine = size_class(count, index)
    theirs = size_class(count_row, index_row)
    ahead = (theirs > mine) | ((theirs == mine) & (index_row < index))
    order = jnp.sum(ahead.astype(F32), axis=1, keepdims=True).astype(I32)
    coded = jnp.where(mine >= 3, 1.0, 0.0) + jnp.where(mine >= 2, 64.0, 0.0)
    coded = jnp.sum(coded + jnp.where(mine >= 1, 4096.0, 0.0)).astype(I32)
    ends = [coded & 63, (coded >> 6) & 63, coded >> 12]
    loads = [jnp.int32(0), jnp.int32(0), jnp.int32(0), jnp.int32(HEAVY_LOAD)]
    taken = [jnp.int32(0), jnp.int32(0), jnp.int32(0), jnp.int32(1)]
    code = jnp.full((GROUPS, 1), 3 * 32, I32)
    for turn in range(GROUPS - 1):
        if plan.sized:
            weight = jnp.where(
                turn < ends[0], 32, jnp.where(turn < ends[1], 16, jnp.where(turn < ends[2], 8, 4))
            )
        else:
            weight = jnp.int32(14)
        first = loads[1] < loads[0]
        last = loads[3] < loads[2]
        low = jnp.where(first, loads[1], loads[0])
        high = jnp.where(last, loads[3], loads[2])
        kind = jnp.where(high < low, jnp.where(last, 3, 2), jnp.where(first, 1, 0))
        place = taken[0]
        for other in range(1, KINDS):
            place = jnp.where(kind == other, taken[other], place)
        for other in range(KINDS):
            chosen = kind == other
            loads[other] = loads[other] + jnp.where(chosen, weight, 0)
            taken[other] = taken[other] + jnp.where(chosen, 1, 0)
        code = jnp.where(order == turn, kind * 32 + place, code)
    return code, unsure


def send_kernel(plan, ids_ref, rows_ref, out_ref, where_ref, my_ids, my_rows, arrived):
    fetch_ids = pltpu.make_async_copy(ids_ref, my_ids, arrived.at[0])
    fetch_rows = pltpu.make_async_copy(rows_ref, my_rows, arrived.at[1])
    fetch_ids.start()
    fetch_rows.start()
    fetch_ids.wait()
    ids = my_ids[...]
    inner = ids & 15
    hit = iota((GROUPS, ROWS), 0) == (ids >> 4)
    code_of_group, unsure = deal(plan, hit.astype(F32))
    code_of_group = code_of_group.astype(F32)
    code = jnp.sum(jnp.where(hit, code_of_group, 0.0), axis=0, keepdims=True).astype(I32)
    kind, place = code >> 5, code & 31
    odd = (place & 1) == 1
    turned_in_last = (place > 0) & ((place < 4) | odd)
    turned_elsewhere = ((place + 1) & 2) == 2
    in_last = kind == KINDS - 1
    turned = (in_last & turned_in_last) | (~in_last & turned_elsewhere)
    chip = kind * 16 + jnp.where(turned, 15 - inner, inner)

    to_chip = (iota((CHIPS, ROWS), 0) == chip).astype(F32)
    earlier = (iota((ROWS, ROWS), 0) < iota((ROWS, ROWS), 1)).astype(BF16)
    rank = jnp.dot(to_chip.astype(BF16), earlier, preferred_element_type=F32)
    slot = jnp.sum(to_chip * rank, axis=0, keepdims=True).astype(I32)
    over = slot >= plan.slots - 1
    flat = jnp.where(over, -1, chip * plan.slots + slot)
    lane = jnp.where(over, -1, (plan.first_lane() + slot) & (LANES - 1))
    where_ref[...] = jnp.concatenate([chip, lane, jnp.zeros((6, ROWS), I32)], axis=0)
    lost = jnp.max(over.astype(F32), axis=1, keepdims=True)
    flag = jnp.maximum(lost, unsure.astype(F32))

    fetch_rows.wait()
    wide = my_rows[...].astype(F32)
    scale = lax.rsqrt(jnp.sum(wide * wide, axis=1, keepdims=True) + 1e-6)
    normed = (wide * scale).astype(BF16)

    at_lane = (iota((LANES, ROWS), 0) == lane).astype(BF16)
    tagged = (to_chip * (place + 1).astype(F32)).astype(BF16)
    tags = lax.dot_general(tagged, at_lane, (((1,), (1,)), ((), ())), preferred_element_type=F32)
    shown = iota((GROUPS, 128), 1) == iota((GROUPS, 128), 0) + 32
    note = jnp.sum(jnp.where(shown, code_of_group, 0.0), axis=0, keepdims=True)
    note = jnp.where(iota((1, 128), 1) == 0, flag, note)
    meta = jnp.concatenate([tags, jnp.broadcast_to(note, (CHIPS, LANES))], axis=1)
    part = plan.held // SEND_PARTS
    blocks = part // plan.slots
    for first in range(0, plan.held, part):
        row = iota((part, ROWS), 0) + first
        out = jnp.dot((row == flat).astype(BF16), normed, preferred_element_type=F32)
        noted = []
        for block in range(blocks):
            end = (block + 1) * plan.slots
            chip_meta = meta[first // plan.slots + block, :][None, :]
            last = jnp.where(iota((8, 2 * LANES), 0) == 7, chip_meta, 0.0)
            noted.append(out[end - plan.slots : end - 8, : 2 * LANES])
            noted.append(out[end - 8 : end, : 2 * LANES] + last)
        noted = jnp.concatenate(noted, axis=0)
        out = jnp.concatenate([noted, out[:, 2 * LANES :]], axis=1)
        out_ref[pl.ds(first, part), :] = out.astype(BF16)


def compact_kernel(plan, held_ref, out_ref, tags_ref, pos_ref, total_ref, tag_ref):
    held = plan.held
    rows = []
    for source in range(CHIPS):
        at = (source + 1) * plan.slots - 1
        tile = held_ref[pl.ds(at // 16 * 16, 16), : 2 * LANES].astype(F32)
        rows.append(tile[at % 16 : at % 16 + 1])
    meta = jnp.concatenate(rows, axis=0)
    tags = meta[:, :LANES]
    note_top = jnp.max(meta[:, LANES:], axis=0, keepdims=True)
    note_low = jnp.min(meta[:, LANES:], axis=0, keepdims=True)
    note_lane = iota((1, 128), 1)
    flag = jnp.where(note_lane == 0, note_top, 0.0)
    flag = jnp.where(note_lane >= 32, note_top - note_low, flag)
    flag = jnp.max(flag, axis=1, keepdims=True)
    count = jnp.sum((tags > 0).astype(F32), axis=1, keepdims=True)
    before = (iota((CHIPS, CHIPS), 1) < iota((CHIPS, CHIPS), 0)).astype(BF16)
    offset = jnp.dot(
        before, jnp.broadcast_to(count, (CHIPS, 128)).astype(BF16), preferred_element_type=F32
    )[:, :1]
    own_block = plan.block_of(iota((CHIPS, held), 1)) == iota((CHIPS, held), 0)
    tag_row = jnp.sum(
        jnp.where(own_block, jnp.concatenate([tags] * (held // LANES), axis=1), 0.0),
        axis=0,
        keepdims=True,
    )
    offset_row = jnp.sum(jnp.where(own_block, offset, 0.0), axis=0, keepdims=True).astype(I32)
    pos = jnp.where(tag_row > 0, offset_row + plan.slot_of(iota((1, held), 1)), -1)
    pos_ref[...] = jnp.broadcast_to(pos, (8, held))
    per_chunk = plan.chunk // plan.slots
    ahead = iota((CHIPS, LANES), 0) - iota((CHIPS, LANES), 1) * per_chunk
    filled = jnp.where((ahead >= 0) & (ahead < per_chunk), count, 0.0)
    filled = jnp.sum(filled, axis=0, keepdims=True)
    total = jnp.sum(filled, axis=1, keepdims=True)
    over = jnp.max(filled, axis=1, keepdims=True) > plan.window - ALIGN
    over = over | (total > plan.capacity)
    source = iota((CHIPS, 1), 0)
    total_ref[pl.ds(0, ALIGN), :] = jnp.zeros((ALIGN, WIDTH), BF16)
    tag_ref[pl.ds(0, ALIGN), :] = jnp.zeros((ALIGN, LANES), BF16)
    base = 0
    chunk = plan.chunk
    for first in range(0, held, chunk):
        if first:
            low = jnp.sum(jnp.where(source == first // plan.slots, offset, 0.0)).astype(I32)
            base = pl.multiple_of((low >> 4) << 4, ALIGN)
        lanes = slice(first, first + chunk)
        take = (iota((plan.window, chunk), 0) + base) == pos[:, lanes]
        part = jnp.dot(take.astype(BF16), held_ref[lanes, :], preferred_element_type=F32)
        tag = jnp.sum(jnp.where(take, tag_row[:, lanes], 0.0), axis=1, keepdims=True)
        tag = jnp.broadcast_to(tag, (plan.window, LANES)).astype(BF16)
        part = part.astype(BF16)
        head, rest = pl.ds(base, ALIGN), pl.ds(base + ALIGN, plan.window - ALIGN)
        total_ref[head, :] += part[:ALIGN]
        total_ref[rest, :] = part[ALIGN:]
        tag_ref[head, :] += tag[:ALIGN]
        tag_ref[rest, :] = tag[ALIGN:]

    def clear(tile, carry):
        rows = pl.ds(pl.multiple_of(tile * ALIGN, ALIGN), ALIGN)
        total_ref[rows, :] = jnp.zeros((ALIGN, WIDTH), BF16)
        tag_ref[rows, :] = jnp.zeros((ALIGN, LANES), BF16)
        return carry

    lax.fori_loop((base + plan.window) >> 4, plan.capacity // ALIGN, clear, 0)
    out_ref[pl.ds(0, plan.capacity), :] = total_ref[pl.ds(0, plan.capacity), :]
    tags = tag_ref[pl.ds(0, plan.capacity), :]
    tags_ref[...] = tags
    one_lane = (iota((TAIL, LANES), 1) == 0).astype(BF16)
    tag_lanes = lax.dot_general(
        one_lane, tags, (((1,), (1,)), ((), ())), preferred_element_type=F32
    )
    flag = jnp.maximum(flag, over.astype(F32))
    note = jnp.where(note_lane == 0, flag, jnp.where(note_lane >= 32, note_top, 0.0))
    note = jnp.concatenate([note, jnp.zeros((1, plan.capacity - LANES), F32)], axis=1)
    tail = jnp.where(iota((TAIL, plan.capacity), 0) < TAIL // 2, note, tag_lanes)
    for first in range(0, plan.capacity, WIDTH):
        piece = tail[:, first : first + WIDTH].astype(BF16)
        out_ref[pl.ds(plan.capacity + first // WIDTH * TAIL, TAIL), : piece.shape[1]] = piece


def tail_of(plan, ref):
    pieces = []
    for first in range(0, plan.capacity, WIDTH):
        rows = pl.ds(plan.capacity + first // WIDTH * TAIL, TAIL)
        pieces.append(ref[rows, : min(WIDTH, plan.capacity - first)].astype(F32))
    tail = jnp.concatenate(pieces, axis=1)
    return tail[:1, :LANES], tail[TAIL // 2 : TAIL // 2 + 1, :]


def score_block(plan, own_ref, tags_ref, rows_ref, row_tags, start, best, same):
    own = own_ref[pl.ds(start, plan.step), :]
    own_tag = tags_ref[pl.ds(start, plan.step), :1].astype(F32)
    for first in range(0, plan.capacity, COLS):
        rows = rows_ref[pl.ds(first, COLS), :]
        scores = lax.dot_general(
            own, rows, (((1,), (1,)), ((), ())), preferred_element_type=F32
        )
        match = own_tag == row_tags[:, first : first + COLS]
        if same:
            index = iota((plan.step, COLS), 0) + (start - first)
            match = match & (index != iota((plan.step, COLS), 1))
        scores = jnp.where(match, scores, -1.0)
        for lane in range(0, COLS, LANES):
            best = jnp.maximum(best, scores[:, lane : lane + LANES])
    return best


def own_kernel(plan, own_ref, tags_ref, out_ref):
    _, own_tags = tail_of(plan, own_ref)
    for start in range(0, plan.capacity, plan.step):
        best = jnp.full((plan.step, LANES), -1.0, F32)
        best = score_block(plan, own_ref, tags_ref, own_ref, own_tags, start, best, True)
        out_ref[pl.ds(start, plan.step), :] = best


def other_kernel(plan, pos_ref, own_ref, tags_ref, other_ref, part_ref, out_ref):
    own_note, _ = tail_of(plan, own_ref)
    other_note, other_tags = tail_of(plan, other_ref)
    note_lane = iota((1, LANES), 1)
    differs = (note_lane >= 32) & (own_note != other_note)
    raised = jnp.where(note_lane == 0, jnp.maximum(own_note, other_note), 0.0)
    flag = jnp.max(jnp.where(differs, 1.0, raised), axis=1, keepdims=True)
    found = [jnp.zeros((8, plan.chunk), F32)] * (plan.held // plan.chunk)
    for start in range(0, plan.capacity, plan.step):
        best = part_ref[pl.ds(start, plan.step), :]
        best = score_block(plan, own_ref, tags_ref, other_ref, other_tags, start, best, False)
        top = jnp.max(best, axis=1, keepdims=True)
        row = iota((plan.step, plan.chunk), 0) + start
        for index in range(plan.reach(start) // plan.chunk, plan.held // plan.chunk):
            pos = pos_ref[0:1, index * plan.chunk : (index + 1) * plan.chunk]
            value = jnp.where(row == pos, top, 0.0)
            found[index] += jnp.sum(value.reshape(plan.step // 8, 8, plan.chunk), axis=0)

    blocks = plan.chunk // plan.slots
    for index, values in enumerate(found):
        lane = iota((1, plan.chunk), 1)
        values = jnp.sum(values, axis=0, keepdims=True)
        values = jnp.where(plan.slot_of(lane) == plan.slots - 1, flag, values)
        in_block = plan.block_of(lane) == iota((blocks, plan.chunk), 0)
        mine = jnp.where(in_block, values, 0.0)
        folded = mine[:, :LANES]
        for first in range(LANES, plan.chunk, LANES):
            folded = folded + mine[:, first : first + LANES]
        out_ref[index * blocks : (index + 1) * blocks, :] = folded


def answer_kernel(plan, where_ref, back_ref, out_ref, flag_ref):
    chip = where_ref[0:1, :]
    lane = where_ref[1:2, :]
    back = back_ref[...]
    to_chip = (iota((CHIPS, ROWS), 0) == chip).astype(BF16)
    high = back.astype(BF16)
    rest = back - high.astype(F32)
    middle = rest.astype(BF16)
    low = (rest - middle.astype(F32)).astype(BF16)
    parts = jnp.concatenate([high, middle, low], axis=1)
    by_row = lax.dot_general(
        parts, to_chip, (((0,), (0,)), ((), ())), preferred_element_type=F32
    )
    by_row = (by_row[:LANES] + by_row[LANES : 2 * LANES]) + by_row[2 * LANES :]
    at_lane = iota((LANES, ROWS), 0) == lane
    out_ref[...] = jnp.sum(jnp.where(at_lane, by_row, 0.0), axis=0, keepdims=True)
    last = iota((CHIPS, LANES), 1) == ((plan.first_lane() + plan.slots - 1) & (LANES - 1))
    flag_ref[0] = (jnp.max(jnp.where(last, back, 0.0)) > 0.0).astype(I32)


VMEM = pl.BlockSpec(memory_space=pltpu.VMEM)
SMEM = pl.BlockSpec(memory_space=pltpu.SMEM)
HBM = pl.BlockSpec(memory_space=pltpu.HBM)


def shape(dims, dtype):
    return jax.ShapeDtypeStruct(dims, dtype)


def call(kernel, plan, name, **options):
    return pl.pallas_call(
        functools.partial(kernel, plan),
        compiler_params=pltpu.CompilerParams(vmem_limit_bytes=48 * 1024 * 1024),
        name=name,
        **options,
    )


def swap(plan, message):
    return lax.all_to_all(message, ("yx", "z"), split_axis=0, concat_axis=0, tiled=True)


def owner_path(plan, embeddings, cluster_ids):
    message, where = call(
        send_kernel,
        plan,
        "send",
        out_shape=(shape((plan.held, WIDTH), BF16), shape((8, ROWS), I32)),
        in_specs=[HBM, HBM],
        out_specs=(VMEM, VMEM),
        scratch_shapes=[
            pltpu.VMEM((1, ROWS), I32),
            pltpu.VMEM((ROWS, WIDTH), BF16),
            pltpu.SemaphoreType.DMA((2,)),
        ],
    )(cluster_ids.reshape(1, ROWS), embeddings)
    held = swap(plan, message)
    packed, tags, pos = call(
        compact_kernel,
        plan,
        "compact",
        out_shape=(
            shape((plan.capacity + plan.tail, WIDTH), BF16),
            shape((plan.capacity, LANES), BF16),
            shape((8, plan.held), I32),
        ),
        in_specs=[VMEM],
        out_specs=(VMEM, VMEM, VMEM),
        scratch_shapes=[
            pltpu.VMEM((plan.held + plan.window, WIDTH), BF16),
            pltpu.VMEM((plan.held + plan.window, LANES), BF16),
        ],
    )(held)
    other = lax.ppermute(packed, "core", [(0, 1), (1, 0)])
    part = call(
        own_kernel,
        plan,
        "score_own",
        out_shape=shape((plan.capacity, LANES), F32),
        in_specs=[VMEM, VMEM],
        out_specs=VMEM,
        cost_estimate=pl.CostEstimate(
            flops=2 * plan.capacity**2 * WIDTH,
            bytes_accessed=2 * plan.capacity * WIDTH,
            transcendentals=0,
        ),
    )(packed, tags)
    best = call(
        other_kernel,
        plan,
        "score_other",
        out_shape=shape((CHIPS, LANES), F32),
        in_specs=[VMEM] * 5,
        out_specs=VMEM,
    )(pos, packed, tags, other, part)
    back = swap(plan, best)
    answer, flag = call(
        answer_kernel,
        plan,
        "answer",
        out_shape=(shape((1, ROWS), F32), shape((1,), I32)),
        in_specs=[VMEM, VMEM],
        out_specs=(VMEM, SMEM),
    )(where, back)
    return answer.reshape(ROWS), flag[0]


def pair_max(left_rows, left_ids, left_pos, right_rows, right_ids, right_pos):
    left_total, width = left_rows.shape
    left_step = min(512, left_total)
    left_count = left_total // left_step

    def left_turn(carry, left_tuple):
        part_rows, part_ids, part_pos = left_tuple
        scores = lax.dot_general(
            part_rows, right_rows, (((1,), (1,)), ((), ())), preferred_element_type=F32
        )
        matches = (
            (part_ids[:, None] == right_ids[None, :])
            & (part_ids[:, None] >= 0)
            & (part_pos[:, None] != right_pos[None, :])
        )
        return carry, jnp.max(jnp.where(matches, scores, -1.0), axis=1)

    _, row_best = lax.scan(
        left_turn,
        0,
        (
            left_rows.reshape(left_count, left_step, width),
            left_ids.reshape(left_count, left_step),
            left_pos.reshape(left_count, left_step),
        ),
    )
    return row_best.reshape(-1)


def gather(piece):
    copies = jnp.broadcast_to(piece[None], (4, *piece.shape))
    whole = lax.all_to_all(copies, "z", split_axis=0, concat_axis=0, tiled=True)
    return whole.reshape(-1, *piece.shape[1:])


def any_path(embeddings, cluster_ids):
    axes = ("yx", "core")
    widened = embeddings.astype(F32)
    normed = (
        widened * lax.rsqrt(jnp.sum(widened * widened, axis=1, keepdims=True) + 1e-06)
    ).astype(BF16)
    owner_group = cluster_ids // CL_GRP
    one_hot = (owner_group[:, None] == jnp.arange(GROUPS, dtype=I32)[None, :]).astype(I32)
    slot_index = jnp.sum(jnp.cumsum(one_hot, axis=0) * one_hot, axis=1) - 1
    flat_slot = owner_group * GROUP_CAP + slot_index
    total = GROUPS * GROUP_CAP
    placement = jnp.arange(total, dtype=I32)[:, None] == flat_slot[None, :]
    outgoing = jnp.dot(placement.astype(BF16), normed, preferred_element_type=F32).astype(BF16)
    outgoing = outgoing.reshape(GROUPS, GROUP_CAP, WIDTH)
    outgoing_ids = jnp.max(jnp.where(placement, cluster_ids[None, :], -1), axis=1)
    outgoing_ids = outgoing_ids.reshape(GROUPS, GROUP_CAP)
    received = lax.all_to_all(outgoing, axes, 0, 0, tiled=True).reshape(total, WIDTH)
    received_ids = lax.all_to_all(outgoing_ids, axes, 0, 0, tiled=True).reshape(total)
    own_pos = jnp.arange(total, dtype=I32) + lax.axis_index("z") * total
    piece_rows = gather(received)
    piece_ids = gather(received_ids)
    piece_pos = jnp.arange(piece_rows.shape[0], dtype=I32)
    best = pair_max(received, received_ids, own_pos, piece_rows, piece_ids, piece_pos)
    best = jnp.maximum(best, -1.0)
    returned = lax.all_to_all(best.reshape(GROUPS, GROUP_CAP), axes, 0, 0, tiled=True)
    return jnp.max(jnp.where(placement, returned.reshape(total)[:, None], -2.0), axis=0)


def unless_done(path, embeddings, cluster_ids, answer, flag):
    def turn(state):
        rows, ids, _, _ = state
        return rows, ids, path(rows, ids), jnp.int32(0)

    embeddings, cluster_ids, answer, flag = lax.optimization_barrier(
        (embeddings, cluster_ids, answer, flag)
    )
    state = (embeddings, cluster_ids, answer, flag)
    return lax.while_loop(lambda state: state[3] > 0, turn, state)[2]


def body(embeddings, cluster_ids):
    def roomy(rows, ids):
        return unless_done(any_path, rows, ids, *owner_path(ROOMY, rows, ids))

    return unless_done(
        roomy, embeddings, cluster_ids, *owner_path(TIGHT, embeddings, cluster_ids)
    )


def solution(mesh):
    chips = Mesh(np.asarray(mesh.devices).reshape(16, 2, 4), ("yx", "core", "z"))
    axes = ("yx", "core", "z")
    return jax.shard_map(
        body, mesh=chips, in_specs=(P(axes, None), P(axes)), out_specs=P(axes), check_vma=False
    )
```

```python
import functools
from typing import NamedTuple

import jax
import jax.numpy as jnp
import numpy as np
from jax import lax
from jax.experimental import pallas as pl
from jax.experimental.pallas import tpu as pltpu
from jax.sharding import Mesh
from jax.sharding import PartitionSpec as P

CL_GRP = 16
GROUPS = 32
GROUP_CAP = 64
WIDTH = 768
ROWS = 512
CHIPS = 64
KINDS = 4
TAIL = 16
LANES = 128
ALIGN = 16
COLS = 256
HEAVY_LOAD = 72
SEND_PARTS = 4

F32 = jnp.float32
BF16 = jnp.bfloat16
I32 = jnp.int32


class Plan(NamedTuple):
    slots: int
    shift: tuple
    chunk: int
    window: int
    capacity: int
    front: int
    step: int
    sized: bool

    @property
    def held(self):
        return CHIPS * self.slots

    @property
    def tail(self):
        return -(-self.capacity // WIDTH) * TAIL

    def reach(self, row):
        return row // (self.chunk // self.slots * (self.slots - 1)) * self.chunk

    def block_of(self, lane):
        return (lane * self.shift[0]) >> self.shift[1]

    def slot_of(self, lane):
        return lane - self.slots * self.block_of(lane)

    def first_lane(self):
        return self.slots * (lax.axis_index("yx") * 4 + lax.axis_index("z"))


TIGHT = Plan(24, (2731, 16), 384, 256, 768, 512, 256, True)
ROOMY = Plan(32, (1, 5), 256, 272, 1280, 768, 256, False)


def iota(shape, dim):
    return lax.broadcasted_iota(I32, shape, dim)


def deal(plan, group_hit):
    count = jnp.sum(group_hit, axis=1, keepdims=True)
    count_row = lax.dot_general(
        jnp.ones((8, ROWS), BF16),
        group_hit.astype(BF16),
        (((1,), (1,)), ((), ())),
        preferred_element_type=F32,
    )[:1]
    index = iota((GROUPS, 1), 0)
    index_row = iota((1, GROUPS), 1)
    full = (count == GROUP_CAP).astype(F32)
    heavy = jnp.sum(full * index.astype(F32), axis=0, keepdims=True).astype(I32)
    unsure = jnp.sum(full, axis=0, keepdims=True) != 1.0
    top = jnp.max(jnp.where(index == heavy, 0.0, count), axis=0, keepdims=True)

    def size_class(sizes, where):
        if plan.sized:
            value = (
                (10 * sizes > 7 * top).astype(I32)
                + (20 * sizes > 7 * top).astype(I32)
                + (50 * sizes > 9 * top).astype(I32)
            )
        else:
            value = jnp.zeros(sizes.shape, I32)
        return jnp.where(where == heavy, -1, value)

    mine = size_class(count, index)
    theirs = size_class(count_row, index_row)
    ahead = (theirs > mine) | ((theirs == mine) & (index_row < index))
    order = jnp.sum(ahead.astype(F32), axis=1, keepdims=True).astype(I32)
    coded = jnp.where(mine >= 3, 1.0, 0.0) + jnp.where(mine >= 2, 64.0, 0.0)
    coded = jnp.sum(coded + jnp.where(mine >= 1, 4096.0, 0.0)).astype(I32)
    ends = [coded & 63, (coded >> 6) & 63, coded >> 12]
    loads = [jnp.int32(0), jnp.int32(0), jnp.int32(0), jnp.int32(HEAVY_LOAD)]
    taken = [jnp.int32(0), jnp.int32(0), jnp.int32(0), jnp.int32(1)]
    code = jnp.full((GROUPS, 1), 3 * 32, I32)
    for turn in range(GROUPS - 1):
        if plan.sized:
            weight = jnp.where(
                turn < ends[0], 32, jnp.where(turn < ends[1], 16, jnp.where(turn < ends[2], 8, 4))
            )
        else:
            weight = jnp.int32(14)
        first = loads[1] < loads[0]
        last = loads[3] < loads[2]
        low = jnp.where(first, loads[1], loads[0])
        high = jnp.where(last, loads[3], loads[2])
        kind = jnp.where(high < low, jnp.where(last, 3, 2), jnp.where(first, 1, 0))
        place = taken[0]
        for other in range(1, KINDS):
            place = jnp.where(kind == other, taken[other], place)
        for other in range(KINDS):
            chosen = kind == other
            loads[other] = loads[other] + jnp.where(chosen, weight, 0)
            taken[other] = taken[other] + jnp.where(chosen, 1, 0)
        code = jnp.where(order == turn, kind * 32 + place, code)
    return code, unsure


def send_kernel(plan, ids_ref, rows_ref, out_ref, where_ref, my_ids, my_rows, arrived):
    fetch_ids = pltpu.make_async_copy(ids_ref, my_ids, arrived.at[0])
    fetch_rows = pltpu.make_async_copy(rows_ref, my_rows, arrived.at[1])
    fetch_ids.start()
    fetch_rows.start()
    fetch_ids.wait()
    ids = my_ids[...]
    inner = ids & 15
    hit = iota((GROUPS, ROWS), 0) == (ids >> 4)
    code_of_group, unsure = deal(plan, hit.astype(F32))
    code_of_group = code_of_group.astype(F32)
    code = jnp.sum(jnp.where(hit, code_of_group, 0.0), axis=0, keepdims=True).astype(I32)
    kind, place = code >> 5, code & 31
    odd = (place & 1) == 1
    turned_in_last = (place > 0) & ((place < 4) | odd)
    turned_elsewhere = ((place + 1) & 2) == 2
    in_last = kind == KINDS - 1
    turned = (in_last & turned_in_last) | (~in_last & turned_elsewhere)
    chip = kind * 16 + jnp.where(turned, 15 - inner, inner)

    to_chip = (iota((CHIPS, ROWS), 0) == chip).astype(F32)
    earlier = (iota((ROWS, ROWS), 0) < iota((ROWS, ROWS), 1)).astype(BF16)
    rank = jnp.dot(to_chip.astype(BF16), earlier, preferred_element_type=F32)
    slot = jnp.sum(to_chip * rank, axis=0, keepdims=True).astype(I32)
    over = slot >= plan.slots - 1
    flat = jnp.where(over, -1, chip * plan.slots + slot)
    lane = jnp.where(over, -1, (plan.first_lane() + slot) & (LANES - 1))
    where_ref[...] = jnp.concatenate([chip, lane, jnp.zeros((6, ROWS), I32)], axis=0)
    lost = jnp.max(over.astype(F32), axis=1, keepdims=True)
    flag = jnp.maximum(lost, unsure.astype(F32))

    fetch_rows.wait()
    wide = my_rows[...].astype(F32)
    scale = lax.rsqrt(jnp.sum(wide * wide, axis=1, keepdims=True) + 1e-6)
    normed = (wide * scale).astype(BF16)

    at_lane = (iota((LANES, ROWS), 0) == lane).astype(BF16)
    tagged = (to_chip * (place + 1).astype(F32)).astype(BF16)
    tags = lax.dot_general(tagged, at_lane, (((1,), (1,)), ((), ())), preferred_element_type=F32)
    shown = iota((GROUPS, 128), 1) == iota((GROUPS, 128), 0) + 32
    note = jnp.sum(jnp.where(shown, code_of_group, 0.0), axis=0, keepdims=True)
    note = jnp.where(iota((1, 128), 1) == 0, flag, note)
    meta = jnp.concatenate([tags, jnp.broadcast_to(note, (CHIPS, LANES))], axis=1)
    part = plan.held // SEND_PARTS
    blocks = part // plan.slots
    for first in range(0, plan.held, part):
        row = iota((part, ROWS), 0) + first
        out = jnp.dot((row == flat).astype(BF16), normed, preferred_element_type=F32)
        noted = []
        for block in range(blocks):
            end = (block + 1) * plan.slots
            chip_meta = meta[first // plan.slots + block, :][None, :]
            last = jnp.where(iota((8, 2 * LANES), 0) == 7, chip_meta, 0.0)
            noted.append(out[end - plan.slots : end - 8, : 2 * LANES])
            noted.append(out[end - 8 : end, : 2 * LANES] + last)
        noted = jnp.concatenate(noted, axis=0)
        out = jnp.concatenate([noted, out[:, 2 * LANES :]], axis=1)
        out_ref[pl.ds(first, part), :] = out.astype(BF16)


def compact_kernel(plan, held_ref, out_ref, back_ref, tags_ref, pos_ref, total_ref, tag_ref):
    held = plan.held
    rows = []
    for source in range(CHIPS):
        at = (source + 1) * plan.slots - 1
        tile = held_ref[pl.ds(at // 16 * 16, 16), : 2 * LANES].astype(F32)
        rows.append(tile[at % 16 : at % 16 + 1])
    meta = jnp.concatenate(rows, axis=0)
    tags = meta[:, :LANES]
    note_top = jnp.max(meta[:, LANES:], axis=0, keepdims=True)
    note_low = jnp.min(meta[:, LANES:], axis=0, keepdims=True)
    note_lane = iota((1, 128), 1)
    flag = jnp.where(note_lane == 0, note_top, 0.0)
    flag = jnp.where(note_lane >= 32, note_top - note_low, flag)
    flag = jnp.max(flag, axis=1, keepdims=True)
    count = jnp.sum((tags > 0).astype(F32), axis=1, keepdims=True)
    before = (iota((CHIPS, CHIPS), 1) < iota((CHIPS, CHIPS), 0)).astype(BF16)
    offset = jnp.dot(
        before, jnp.broadcast_to(count, (CHIPS, 128)).astype(BF16), preferred_element_type=F32
    )[:, :1]
    own_block = plan.block_of(iota((CHIPS, held), 1)) == iota((CHIPS, held), 0)
    tag_row = jnp.sum(
        jnp.where(own_block, jnp.concatenate([tags] * (held // LANES), axis=1), 0.0),
        axis=0,
        keepdims=True,
    )
    offset_row = jnp.sum(jnp.where(own_block, offset, 0.0), axis=0, keepdims=True).astype(I32)
    pos = jnp.where(tag_row > 0, offset_row + plan.slot_of(iota((1, held), 1)), -1)
    pos_ref[...] = jnp.broadcast_to(pos, (8, held))
    per_chunk = plan.chunk // plan.slots
    ahead = iota((CHIPS, LANES), 0) - iota((CHIPS, LANES), 1) * per_chunk
    filled = jnp.where((ahead >= 0) & (ahead < per_chunk), count, 0.0)
    filled = jnp.sum(filled, axis=0, keepdims=True)
    total = jnp.sum(filled, axis=1, keepdims=True)
    over = jnp.max(filled, axis=1, keepdims=True) > plan.window - ALIGN
    over = over | (total > plan.capacity)
    source = iota((CHIPS, 1), 0)
    total_ref[pl.ds(0, ALIGN), :] = jnp.zeros((ALIGN, WIDTH), BF16)
    tag_ref[pl.ds(0, ALIGN), :] = jnp.zeros((ALIGN, LANES), BF16)
    base = 0
    chunk = plan.chunk
    for first in range(0, held, chunk):
        if first:
            low = jnp.sum(jnp.where(source == first // plan.slots, offset, 0.0)).astype(I32)
            base = pl.multiple_of((low >> 4) << 4, ALIGN)
        lanes = slice(first, first + chunk)
        take = (iota((plan.window, chunk), 0) + base) == pos[:, lanes]
        part = jnp.dot(take.astype(BF16), held_ref[lanes, :], preferred_element_type=F32)
        tag = jnp.sum(jnp.where(take, tag_row[:, lanes], 0.0), axis=1, keepdims=True)
        tag = jnp.broadcast_to(tag, (plan.window, LANES)).astype(BF16)
        part = part.astype(BF16)
        head, rest = pl.ds(base, ALIGN), pl.ds(base + ALIGN, plan.window - ALIGN)
        total_ref[head, :] += part[:ALIGN]
        total_ref[rest, :] = part[ALIGN:]
        tag_ref[head, :] += tag[:ALIGN]
        tag_ref[rest, :] = tag[ALIGN:]

    def clear(tile, carry):
        rows = pl.ds(pl.multiple_of(tile * ALIGN, ALIGN), ALIGN)
        total_ref[rows, :] = jnp.zeros((ALIGN, WIDTH), BF16)
        tag_ref[rows, :] = jnp.zeros((ALIGN, LANES), BF16)
        return carry

    lax.fori_loop((base + plan.window) >> 4, plan.capacity // ALIGN, clear, 0)
    out_ref[pl.ds(0, plan.front), :] = total_ref[pl.ds(0, plan.front), :]
    back_ref[...] = total_ref[pl.ds(plan.front, plan.capacity - plan.front), :]
    tags = tag_ref[pl.ds(0, plan.capacity), :]
    tags_ref[...] = tags
    one_lane = (iota((TAIL, LANES), 1) == 0).astype(BF16)
    tag_lanes = lax.dot_general(
        one_lane, tags, (((1,), (1,)), ((), ())), preferred_element_type=F32
    )
    flag = jnp.maximum(flag, over.astype(F32))
    note = jnp.where(note_lane == 0, flag, jnp.where(note_lane >= 32, note_top, 0.0))
    note = jnp.concatenate([note, jnp.zeros((1, plan.capacity - LANES), F32)], axis=1)
    tail = jnp.where(iota((TAIL, plan.capacity), 0) < TAIL // 2, note, tag_lanes)
    for first in range(0, plan.capacity, WIDTH):
        piece = tail[:, first : first + WIDTH].astype(BF16)
        out_ref[pl.ds(plan.front + first // WIDTH * TAIL, TAIL), : piece.shape[1]] = piece


def tail_of(plan, ref):
    pieces = []
    for first in range(0, plan.capacity, WIDTH):
        rows = pl.ds(plan.front + first // WIDTH * TAIL, TAIL)
        pieces.append(ref[rows, : min(WIDTH, plan.capacity - first)].astype(F32))
    tail = jnp.concatenate(pieces, axis=1)
    return tail[:1, :LANES], tail[TAIL // 2 : TAIL // 2 + 1, :]


def score_block(plan, own_refs, tags_ref, rows_ref, count, offset, row_tags, start, best, same):
    inside = start - plan.front
    own_ref, at = (own_refs[0], start) if inside < 0 else (own_refs[1], inside)
    own = own_ref[pl.ds(at, plan.step), :]
    own_tag = tags_ref[pl.ds(start, plan.step), :1].astype(F32)
    for first in range(0, count, COLS):
        rows = rows_ref[pl.ds(first, COLS), :]
        scores = lax.dot_general(
            own, rows, (((1,), (1,)), ((), ())), preferred_element_type=F32
        )
        match = own_tag == row_tags[:, offset + first : offset + first + COLS]
        if same:
            index = iota((plan.step, COLS), 0) + (start - offset - first)
            match = match & (index != iota((plan.step, COLS), 1))
        scores = jnp.where(match, scores, -1.0)
        for lane in range(0, COLS, LANES):
            best = jnp.maximum(best, scores[:, lane : lane + LANES])
    return best


def own_kernel(plan, front_ref, back_ref, tags_ref, out_ref):
    _, tags = tail_of(plan, front_ref)
    own = (front_ref, back_ref)
    rest = plan.capacity - plan.front
    for start in range(0, plan.capacity, plan.step):
        best = jnp.full((plan.step, LANES), -1.0, F32)
        best = score_block(
            plan, own, tags_ref, front_ref, plan.front, 0, tags, start, best, True
        )
        best = score_block(
            plan, own, tags_ref, back_ref, rest, plan.front, tags, start, best, True
        )
        out_ref[pl.ds(start, plan.step), :] = best


def first_kernel(plan, front_ref, back_ref, tags_ref, other_ref, part_ref, out_ref):
    _, tags = tail_of(plan, other_ref)
    own = (front_ref, back_ref)
    for start in range(0, plan.capacity, plan.step):
        best = part_ref[pl.ds(start, plan.step), :]
        best = score_block(
            plan, own, tags_ref, other_ref, plan.front, 0, tags, start, best, False
        )
        out_ref[pl.ds(start, plan.step), :] = best


def other_kernel(
    plan, pos_ref, front_ref, back_ref, tags_ref, other_ref, last_ref, part_ref, out_ref
):
    own_note, _ = tail_of(plan, front_ref)
    other_note, other_tags = tail_of(plan, other_ref)
    note_lane = iota((1, LANES), 1)
    differs = (note_lane >= 32) & (own_note != other_note)
    raised = jnp.where(note_lane == 0, jnp.maximum(own_note, other_note), 0.0)
    flag = jnp.max(jnp.where(differs, 1.0, raised), axis=1, keepdims=True)
    found = [jnp.zeros((8, plan.chunk), F32)] * (plan.held // plan.chunk)
    own = (front_ref, back_ref)
    rest = plan.capacity - plan.front
    for start in range(0, plan.capacity, plan.step):
        best = part_ref[pl.ds(start, plan.step), :]
        best = score_block(
            plan, own, tags_ref, last_ref, rest, plan.front, other_tags, start, best, False
        )
        top = jnp.max(best, axis=1, keepdims=True)
        row = iota((plan.step, plan.chunk), 0) + start
        for index in range(plan.reach(start) // plan.chunk, plan.held // plan.chunk):
            pos = pos_ref[0:1, index * plan.chunk : (index + 1) * plan.chunk]
            value = jnp.where(row == pos, top, 0.0)
            found[index] += jnp.sum(value.reshape(plan.step // 8, 8, plan.chunk), axis=0)

    blocks = plan.chunk // plan.slots
    for index, values in enumerate(found):
        lane = iota((1, plan.chunk), 1)
        values = jnp.sum(values, axis=0, keepdims=True)
        values = jnp.where(plan.slot_of(lane) == plan.slots - 1, flag, values)
        in_block = plan.block_of(lane) == iota((blocks, plan.chunk), 0)
        mine = jnp.where(in_block, values, 0.0)
        folded = mine[:, :LANES]
        for first in range(LANES, plan.chunk, LANES):
            folded = folded + mine[:, first : first + LANES]
        out_ref[index * blocks : (index + 1) * blocks, :] = folded


def answer_kernel(plan, where_ref, back_ref, out_ref, flag_ref):
    chip = where_ref[0:1, :]
    lane = where_ref[1:2, :]
    back = back_ref[...]
    to_chip = (iota((CHIPS, ROWS), 0) == chip).astype(BF16)
    high = back.astype(BF16)
    rest = back - high.astype(F32)
    middle = rest.astype(BF16)
    low = (rest - middle.astype(F32)).astype(BF16)
    parts = jnp.concatenate([high, middle, low], axis=1)
    by_row = lax.dot_general(
        parts, to_chip, (((0,), (0,)), ((), ())), preferred_element_type=F32
    )
    by_row = (by_row[:LANES] + by_row[LANES : 2 * LANES]) + by_row[2 * LANES :]
    at_lane = iota((LANES, ROWS), 0) == lane
    out_ref[...] = jnp.sum(jnp.where(at_lane, by_row, 0.0), axis=0, keepdims=True)
    last = iota((CHIPS, LANES), 1) == ((plan.first_lane() + plan.slots - 1) & (LANES - 1))
    flag_ref[0] = (jnp.max(jnp.where(last, back, 0.0)) > 0.0).astype(I32)


VMEM = pl.BlockSpec(memory_space=pltpu.VMEM)
SMEM = pl.BlockSpec(memory_space=pltpu.SMEM)
HBM = pl.BlockSpec(memory_space=pltpu.HBM)


def shape(dims, dtype):
    return jax.ShapeDtypeStruct(dims, dtype)


def call(kernel, plan, name, **options):
    return pl.pallas_call(
        functools.partial(kernel, plan),
        compiler_params=pltpu.CompilerParams(vmem_limit_bytes=48 * 1024 * 1024),
        name=name,
        **options,
    )


def swap(plan, message):
    return lax.all_to_all(message, ("yx", "z"), split_axis=0, concat_axis=0, tiled=True)


def owner_path(plan, embeddings, cluster_ids):
    message, where = call(
        send_kernel,
        plan,
        "send",
        out_shape=(shape((plan.held, WIDTH), BF16), shape((8, ROWS), I32)),
        in_specs=[HBM, HBM],
        out_specs=(VMEM, VMEM),
        scratch_shapes=[
            pltpu.VMEM((1, ROWS), I32),
            pltpu.VMEM((ROWS, WIDTH), BF16),
            pltpu.SemaphoreType.DMA((2,)),
        ],
    )(cluster_ids.reshape(1, ROWS), embeddings)
    held = swap(plan, message)
    front, rear, tags, pos = call(
        compact_kernel,
        plan,
        "compact",
        out_shape=(
            shape((plan.front + plan.tail, WIDTH), BF16),
            shape((plan.capacity - plan.front, WIDTH), BF16),
            shape((plan.capacity, LANES), BF16),
            shape((8, plan.held), I32),
        ),
        in_specs=[VMEM],
        out_specs=(VMEM,) * 4,
        scratch_shapes=[
            pltpu.VMEM((plan.held + plan.window, WIDTH), BF16),
            pltpu.VMEM((plan.held + plan.window, LANES), BF16),
        ],
    )(held)
    pairs = [(0, 1), (1, 0)]
    other_front = lax.ppermute(front, "core", pairs)
    other_rear = lax.ppermute(rear, "core", pairs)
    part = call(
        own_kernel,
        plan,
        "score_own",
        out_shape=shape((plan.capacity, LANES), F32),
        in_specs=[VMEM] * 3,
        out_specs=VMEM,
        cost_estimate=pl.CostEstimate(
            flops=2 * plan.capacity**2 * WIDTH,
            bytes_accessed=2 * plan.capacity * WIDTH,
            transcendentals=0,
        ),
    )(front, rear, tags)
    part = call(
        first_kernel,
        plan,
        "score_first",
        out_shape=shape((plan.capacity, LANES), F32),
        in_specs=[VMEM] * 5,
        out_specs=VMEM,
        cost_estimate=pl.CostEstimate(
            flops=2 * plan.capacity * plan.front * WIDTH,
            bytes_accessed=2 * plan.capacity * WIDTH,
            transcendentals=0,
        ),
    )(front, rear, tags, other_front, part)
    best = call(
        other_kernel,
        plan,
        "score_other",
        out_shape=shape((CHIPS, LANES), F32),
        in_specs=[VMEM] * 7,
        out_specs=VMEM,
    )(pos, front, rear, tags, other_front, other_rear, part)
    back = swap(plan, best)
    answer, flag = call(
        answer_kernel,
        plan,
        "answer",
        out_shape=(shape((1, ROWS), F32), shape((1,), I32)),
        in_specs=[VMEM, VMEM],
        out_specs=(VMEM, SMEM),
    )(where, back)
    return answer.reshape(ROWS), flag[0]


def pair_max(left_rows, left_ids, left_pos, right_rows, right_ids, right_pos):
    left_total, width = left_rows.shape
    left_step = min(512, left_total)
    left_count = left_total // left_step

    def left_turn(carry, left_tuple):
        part_rows, part_ids, part_pos = left_tuple
        scores = lax.dot_general(
            part_rows, right_rows, (((1,), (1,)), ((), ())), preferred_element_type=F32
        )
        matches = (
            (part_ids[:, None] == right_ids[None, :])
            & (part_ids[:, None] >= 0)
            & (part_pos[:, None] != right_pos[None, :])
        )
        return carry, jnp.max(jnp.where(matches, scores, -1.0), axis=1)

    _, row_best = lax.scan(
        left_turn,
        0,
        (
            left_rows.reshape(left_count, left_step, width),
            left_ids.reshape(left_count, left_step),
            left_pos.reshape(left_count, left_step),
        ),
    )
    return row_best.reshape(-1)


def gather(piece):
    copies = jnp.broadcast_to(piece[None], (4, *piece.shape))
    whole = lax.all_to_all(copies, "z", split_axis=0, concat_axis=0, tiled=True)
    return whole.reshape(-1, *piece.shape[1:])


def any_path(embeddings, cluster_ids):
    axes = ("yx", "core")
    widened = embeddings.astype(F32)
    normed = (
        widened * lax.rsqrt(jnp.sum(widened * widened, axis=1, keepdims=True) + 1e-06)
    ).astype(BF16)
    owner_group = cluster_ids // CL_GRP
    one_hot = (owner_group[:, None] == jnp.arange(GROUPS, dtype=I32)[None, :]).astype(I32)
    slot_index = jnp.sum(jnp.cumsum(one_hot, axis=0) * one_hot, axis=1) - 1
    flat_slot = owner_group * GROUP_CAP + slot_index
    total = GROUPS * GROUP_CAP
    placement = jnp.arange(total, dtype=I32)[:, None] == flat_slot[None, :]
    outgoing = jnp.dot(placement.astype(BF16), normed, preferred_element_type=F32).astype(BF16)
    outgoing = outgoing.reshape(GROUPS, GROUP_CAP, WIDTH)
    outgoing_ids = jnp.max(jnp.where(placement, cluster_ids[None, :], -1), axis=1)
    outgoing_ids = outgoing_ids.reshape(GROUPS, GROUP_CAP)
    received = lax.all_to_all(outgoing, axes, 0, 0, tiled=True).reshape(total, WIDTH)
    received_ids = lax.all_to_all(outgoing_ids, axes, 0, 0, tiled=True).reshape(total)
    own_pos = jnp.arange(total, dtype=I32) + lax.axis_index("z") * total
    piece_rows = gather(received)
    piece_ids = gather(received_ids)
    piece_pos = jnp.arange(piece_rows.shape[0], dtype=I32)
    best = pair_max(received, received_ids, own_pos, piece_rows, piece_ids, piece_pos)
    best = jnp.maximum(best, -1.0)
    returned = lax.all_to_all(best.reshape(GROUPS, GROUP_CAP), axes, 0, 0, tiled=True)
    return jnp.max(jnp.where(placement, returned.reshape(total)[:, None], -2.0), axis=0)


def unless_done(path, embeddings, cluster_ids, answer, flag):
    def turn(state):
        rows, ids, _, _ = state
        return rows, ids, path(rows, ids), jnp.int32(0)

    embeddings, cluster_ids, answer, flag = lax.optimization_barrier(
        (embeddings, cluster_ids, answer, flag)
    )
    state = (embeddings, cluster_ids, answer, flag)
    return lax.while_loop(lambda state: state[3] > 0, turn, state)[2]


def body(embeddings, cluster_ids):
    def roomy(rows, ids):
        return unless_done(any_path, rows, ids, *owner_path(ROOMY, rows, ids))

    return unless_done(
        roomy, embeddings, cluster_ids, *owner_path(TIGHT, embeddings, cluster_ids)
    )


def solution(mesh):
    chips = Mesh(np.asarray(mesh.devices).reshape(16, 2, 4), ("yx", "core", "z"))
    axes = ("yx", "core", "z")
    return jax.shard_map(
        body, mesh=chips, in_specs=(P(axes, None), P(axes)), out_specs=P(axes), check_vma=False
    )
```

```python
import functools
from typing import NamedTuple

import jax
import jax.numpy as jnp
import numpy as np
from jax import lax
from jax.experimental import pallas as pl
from jax.experimental.pallas import tpu as pltpu
from jax.sharding import Mesh
from jax.sharding import PartitionSpec as P

CL_GRP = 16
GROUPS = 32
GROUP_CAP = 64
WIDTH = 768
ROWS = 512
CHIPS = 64
KINDS = 4
TAIL = 16
LANES = 128
ALIGN = 16
COLS = 256
HEAVY_LOAD = 72
SEND_PARTS = 4

F32 = jnp.float32
BF16 = jnp.bfloat16
I32 = jnp.int32


class Plan(NamedTuple):
    slots: int
    shift: tuple
    chunk: int
    window: int
    capacity: int
    step: int
    sized: bool

    @property
    def held(self):
        return CHIPS * self.slots

    @property
    def tail(self):
        return -(-self.capacity // WIDTH) * TAIL

    def reach(self, row):
        return row // (self.chunk // self.slots * (self.slots - 1)) * self.chunk

    def block_of(self, lane):
        return (lane * self.shift[0]) >> self.shift[1]

    def slot_of(self, lane):
        return lane - self.slots * self.block_of(lane)

    def first_lane(self):
        return self.slots * (lax.axis_index("yx") * 4 + lax.axis_index("z"))


TIGHT = Plan(24, (2731, 16), 384, 256, 768, 384, True)
ROOMY = Plan(32, (1, 5), 256, 272, 1280, 320, False)


def iota(shape, dim):
    return lax.broadcasted_iota(I32, shape, dim)


def deal(plan, group_hit):
    count = jnp.sum(group_hit, axis=1, keepdims=True)
    count_row = lax.dot_general(
        jnp.ones((8, ROWS), BF16),
        group_hit.astype(BF16),
        (((1,), (1,)), ((), ())),
        preferred_element_type=F32,
    )[:1]
    index = iota((GROUPS, 1), 0)
    index_row = iota((1, GROUPS), 1)
    full = (count == GROUP_CAP).astype(F32)
    heavy = jnp.sum(full * index.astype(F32), axis=0, keepdims=True).astype(I32)
    unsure = jnp.sum(full, axis=0, keepdims=True) != 1.0
    top = jnp.max(jnp.where(index == heavy, 0.0, count), axis=0, keepdims=True)

    def size_class(sizes, where):
        if plan.sized:
            value = (
                (10 * sizes > 7 * top).astype(I32)
                + (20 * sizes > 7 * top).astype(I32)
                + (50 * sizes > 9 * top).astype(I32)
            )
        else:
            value = jnp.zeros(sizes.shape, I32)
        return jnp.where(where == heavy, -1, value)

    mine = size_class(count, index)
    theirs = size_class(count_row, index_row)
    ahead = (theirs > mine) | ((theirs == mine) & (index_row < index))
    order = jnp.sum(ahead.astype(F32), axis=1, keepdims=True).astype(I32)
    coded = jnp.where(mine >= 3, 1.0, 0.0) + jnp.where(mine >= 2, 64.0, 0.0)
    coded = coded + jnp.where(mine >= 1, 4096.0, 0.0)
    coded = jnp.sum(coded, axis=0, keepdims=True).astype(I32)[0, 0]
    ends = [coded & 63, (coded >> 6) & 63, coded >> 12]
    states = [jnp.int32(kind) for kind in range(KINDS - 1)]
    states.append(jnp.int32((HEAVY_LOAD << 8) + (1 << 2) + KINDS - 1))
    picked = jnp.full((GROUPS, 1), KINDS - 1, I32)
    for turn in range(GROUPS - 1):
        if plan.sized:
            weight = jnp.where(
                turn < ends[0], 32, jnp.where(turn < ends[1], 16, jnp.where(turn < ends[2], 8, 4))
            )
        else:
            weight = jnp.int32(14)
        least = jnp.minimum(
            jnp.minimum(states[0], states[1]), jnp.minimum(states[2], states[3])
        )
        step = (weight << 8) + (1 << 2)
        states = [jnp.where(state == least, state + step, state) for state in states]
        picked = jnp.where(order == turn, least, picked)
    code = (picked & 3) * 32 + ((picked >> 2) & 63)
    return code, unsure


def send_kernel(plan, ids_ref, rows_ref, out_ref, where_ref, my_ids, my_rows, arrived):
    fetch_ids = pltpu.make_async_copy(ids_ref, my_ids, arrived.at[0])
    fetch_rows = pltpu.make_async_copy(rows_ref, my_rows, arrived.at[1])
    fetch_ids.start()
    fetch_rows.start()
    fetch_ids.wait()
    ids = my_ids[...]
    inner = ids & 15
    hit = iota((GROUPS, ROWS), 0) == (ids >> 4)
    code_of_group, unsure = deal(plan, hit.astype(F32))
    code_of_group = code_of_group.astype(F32)
    code = jnp.sum(jnp.where(hit, code_of_group, 0.0), axis=0, keepdims=True).astype(I32)
    kind, place = code >> 5, code & 31
    odd = (place & 1) == 1
    turned_in_last = (place > 0) & ((place < 4) | odd)
    turned_elsewhere = ((place + 1) & 2) == 2
    in_last = kind == KINDS - 1
    turned = (in_last & turned_in_last) | (~in_last & turned_elsewhere)
    chip = kind * 16 + jnp.where(turned, 15 - inner, inner)

    to_chip = (iota((CHIPS, ROWS), 0) == chip).astype(F32)
    earlier = (iota((ROWS, ROWS), 0) < iota((ROWS, ROWS), 1)).astype(BF16)
    rank = jnp.dot(to_chip.astype(BF16), earlier, preferred_element_type=F32)
    slot = jnp.sum(to_chip * rank, axis=0, keepdims=True).astype(I32)
    over = slot >= plan.slots - 1
    flat = jnp.where(over, -1, chip * plan.slots + slot)
    lane = jnp.where(over, -1, (plan.first_lane() + slot) & (LANES - 1))
    where_ref[...] = jnp.concatenate([chip, lane, jnp.zeros((6, ROWS), I32)], axis=0)
    lost = jnp.max(over.astype(F32), axis=1, keepdims=True)
    flag = jnp.maximum(lost, unsure.astype(F32))

    fetch_rows.wait()
    wide = my_rows[...].astype(F32)
    scale = lax.rsqrt(jnp.sum(wide * wide, axis=1, keepdims=True) + 1e-6)
    normed = (wide * scale).astype(BF16)

    at_lane = (iota((LANES, ROWS), 0) == lane).astype(BF16)
    tagged = (to_chip * (place + 1).astype(F32)).astype(BF16)
    tags = lax.dot_general(tagged, at_lane, (((1,), (1,)), ((), ())), preferred_element_type=F32)
    shown = iota((GROUPS, 128), 1) == iota((GROUPS, 128), 0) + 32
    note = jnp.sum(jnp.where(shown, code_of_group, 0.0), axis=0, keepdims=True)
    note = jnp.where(iota((1, 128), 1) == 0, flag, note)
    meta = jnp.concatenate([tags, jnp.broadcast_to(note, (CHIPS, LANES))], axis=1)
    part = plan.held // SEND_PARTS
    blocks = part // plan.slots
    for first in range(0, plan.held, part):
        row = iota((part, ROWS), 0) + first
        out = jnp.dot((row == flat).astype(BF16), normed, preferred_element_type=F32)
        noted = []
        for block in range(blocks):
            end = (block + 1) * plan.slots
            chip_meta = meta[first // plan.slots + block, :][None, :]
            last = jnp.where(iota((8, 2 * LANES), 0) == 7, chip_meta, 0.0)
            noted.append(out[end - plan.slots : end - 8, : 2 * LANES])
            noted.append(out[end - 8 : end, : 2 * LANES] + last)
        noted = jnp.concatenate(noted, axis=0)
        out = jnp.concatenate([noted, out[:, 2 * LANES :]], axis=1)
        out_ref[pl.ds(first, part), :] = out.astype(BF16)


def compact_kernel(plan, held_ref, out_ref, tags_ref, pos_ref, total_ref, tag_ref):
    held = plan.held
    rows = []
    for source in range(CHIPS):
        at = (source + 1) * plan.slots - 1
        tile = held_ref[pl.ds(at // 16 * 16, 16), : 2 * LANES].astype(F32)
        rows.append(tile[at % 16 : at % 16 + 1])
    meta = jnp.concatenate(rows, axis=0)
    tags = meta[:, :LANES]
    note_top = jnp.max(meta[:, LANES:], axis=0, keepdims=True)
    note_low = jnp.min(meta[:, LANES:], axis=0, keepdims=True)
    note_lane = iota((1, 128), 1)
    flag = jnp.where(note_lane == 0, note_top, 0.0)
    flag = jnp.where(note_lane >= 32, note_top - note_low, flag)
    flag = jnp.max(flag, axis=1, keepdims=True)
    count = jnp.sum((tags > 0).astype(F32), axis=1, keepdims=True)
    before = (iota((CHIPS, CHIPS), 1) < iota((CHIPS, CHIPS), 0)).astype(BF16)
    offset = jnp.dot(
        before, jnp.broadcast_to(count, (CHIPS, 128)).astype(BF16), preferred_element_type=F32
    )[:, :1]
    own_block = plan.block_of(iota((CHIPS, held), 1)) == iota((CHIPS, held), 0)
    tag_row = jnp.sum(
        jnp.where(own_block, jnp.concatenate([tags] * (held // LANES), axis=1), 0.0),
        axis=0,
        keepdims=True,
    )
    offset_row = jnp.sum(jnp.where(own_block, offset, 0.0), axis=0, keepdims=True).astype(I32)
    pos = jnp.where(tag_row > 0, offset_row + plan.slot_of(iota((1, held), 1)), -1)
    pos_ref[...] = jnp.broadcast_to(pos, (8, held))
    per_chunk = plan.chunk // plan.slots
    ahead = iota((CHIPS, LANES), 0) - iota((CHIPS, LANES), 1) * per_chunk
    filled = jnp.where((ahead >= 0) & (ahead < per_chunk), count, 0.0)
    filled = jnp.sum(filled, axis=0, keepdims=True)
    total = jnp.sum(filled, axis=1, keepdims=True)
    over = jnp.max(filled, axis=1, keepdims=True) > plan.window - ALIGN
    over = over | (total > plan.capacity)
    source = iota((CHIPS, 1), 0)
    total_ref[pl.ds(0, ALIGN), :] = jnp.zeros((ALIGN, WIDTH), BF16)
    tag_ref[pl.ds(0, ALIGN), :] = jnp.zeros((ALIGN, LANES), BF16)
    base = 0
    chunk = plan.chunk
    for first in range(0, held, chunk):
        if first:
            low = jnp.sum(jnp.where(source == first // plan.slots, offset, 0.0)).astype(I32)
            base = pl.multiple_of((low >> 4) << 4, ALIGN)
        lanes = slice(first, first + chunk)
        take = (iota((plan.window, chunk), 0) + base) == pos[:, lanes]
        part = jnp.dot(take.astype(BF16), held_ref[lanes, :], preferred_element_type=F32)
        tag = jnp.sum(jnp.where(take, tag_row[:, lanes], 0.0), axis=1, keepdims=True)
        tag = jnp.broadcast_to(tag, (plan.window, LANES)).astype(BF16)
        part = part.astype(BF16)
        head, rest = pl.ds(base, ALIGN), pl.ds(base + ALIGN, plan.window - ALIGN)
        total_ref[head, :] += part[:ALIGN]
        total_ref[rest, :] = part[ALIGN:]
        tag_ref[head, :] += tag[:ALIGN]
        tag_ref[rest, :] = tag[ALIGN:]

    def clear(tile, carry):
        rows = pl.ds(pl.multiple_of(tile * ALIGN, ALIGN), ALIGN)
        total_ref[rows, :] = jnp.zeros((ALIGN, WIDTH), BF16)
        tag_ref[rows, :] = jnp.zeros((ALIGN, LANES), BF16)
        return carry

    lax.fori_loop((base + plan.window) >> 4, plan.capacity // ALIGN, clear, 0)
    out_ref[pl.ds(0, plan.capacity), :] = total_ref[pl.ds(0, plan.capacity), :]
    tags = tag_ref[pl.ds(0, plan.capacity), :]
    tags_ref[...] = tags
    one_lane = (iota((TAIL, LANES), 1) == 0).astype(BF16)
    tag_lanes = lax.dot_general(
        one_lane, tags, (((1,), (1,)), ((), ())), preferred_element_type=F32
    )
    flag = jnp.maximum(flag, over.astype(F32))
    note = jnp.where(note_lane == 0, flag, jnp.where(note_lane >= 32, note_top, 0.0))
    note = jnp.concatenate([note, jnp.zeros((1, plan.capacity - LANES), F32)], axis=1)
    tail = jnp.where(iota((TAIL, plan.capacity), 0) < TAIL // 2, note, tag_lanes)
    for first in range(0, plan.capacity, WIDTH):
        piece = tail[:, first : first + WIDTH].astype(BF16)
        out_ref[pl.ds(plan.capacity + first // WIDTH * TAIL, TAIL), : piece.shape[1]] = piece


def tail_of(plan, ref):
    pieces = []
    for first in range(0, plan.capacity, WIDTH):
        rows = pl.ds(plan.capacity + first // WIDTH * TAIL, TAIL)
        pieces.append(ref[rows, : min(WIDTH, plan.capacity - first)].astype(F32))
    tail = jnp.concatenate(pieces, axis=1)
    return tail[:1, :LANES], tail[TAIL // 2 : TAIL // 2 + 1, :]


def score_block(plan, own_ref, tags_ref, rows_ref, row_tags, start, best, same):
    own = own_ref[pl.ds(start, plan.step), :]
    own_tag = tags_ref[pl.ds(start, plan.step), :1].astype(F32)
    for first in range(0, plan.capacity, COLS):
        rows = rows_ref[pl.ds(first, COLS), :]
        scores = lax.dot_general(
            own, rows, (((1,), (1,)), ((), ())), preferred_element_type=F32
        )
        match = own_tag == row_tags[:, first : first + COLS]
        if same:
            index = iota((plan.step, COLS), 0) + (start - first)
            match = match & (index != iota((plan.step, COLS), 1))
        scores = jnp.where(match, scores, -1.0)
        for lane in range(0, COLS, LANES):
            best = jnp.maximum(best, scores[:, lane : lane + LANES])
    return best


def own_kernel(plan, own_ref, tags_ref, out_ref):
    _, own_tags = tail_of(plan, own_ref)
    for start in range(0, plan.capacity, plan.step):
        best = jnp.full((plan.step, LANES), -1.0, F32)
        best = score_block(plan, own_ref, tags_ref, own_ref, own_tags, start, best, True)
        out_ref[pl.ds(start, plan.step), :] = best


def other_kernel(plan, pos_ref, own_ref, tags_ref, other_ref, part_ref, out_ref):
    own_note, _ = tail_of(plan, own_ref)
    other_note, other_tags = tail_of(plan, other_ref)
    note_lane = iota((1, LANES), 1)
    differs = (note_lane >= 32) & (own_note != other_note)
    raised = jnp.where(note_lane == 0, jnp.maximum(own_note, other_note), 0.0)
    flag = jnp.max(jnp.where(differs, 1.0, raised), axis=1, keepdims=True)
    found = [jnp.zeros((8, plan.chunk), F32)] * (plan.held // plan.chunk)
    for start in range(0, plan.capacity, plan.step):
        best = part_ref[pl.ds(start, plan.step), :]
        best = score_block(plan, own_ref, tags_ref, other_ref, other_tags, start, best, False)
        top = jnp.max(best, axis=1, keepdims=True)
        row = iota((plan.step, plan.chunk), 0) + start
        for index in range(plan.reach(start) // plan.chunk, plan.held // plan.chunk):
            pos = pos_ref[0:1, index * plan.chunk : (index + 1) * plan.chunk]
            value = jnp.where(row == pos, top, 0.0)
            found[index] += jnp.sum(value.reshape(plan.step // 8, 8, plan.chunk), axis=0)

    blocks = plan.chunk // plan.slots
    for index, values in enumerate(found):
        lane = iota((1, plan.chunk), 1)
        values = jnp.sum(values, axis=0, keepdims=True)
        values = jnp.where(plan.slot_of(lane) == plan.slots - 1, flag, values)
        in_block = plan.block_of(lane) == iota((blocks, plan.chunk), 0)
        mine = jnp.where(in_block, values, 0.0)
        folded = mine[:, :LANES]
        for first in range(LANES, plan.chunk, LANES):
            folded = folded + mine[:, first : first + LANES]
        out_ref[index * blocks : (index + 1) * blocks, :] = folded


def answer_kernel(plan, where_ref, back_ref, out_ref, flag_ref):
    chip = where_ref[0:1, :]
    lane = where_ref[1:2, :]
    back = back_ref[...]
    to_chip = (iota((CHIPS, ROWS), 0) == chip).astype(BF16)
    high = back.astype(BF16)
    rest = back - high.astype(F32)
    middle = rest.astype(BF16)
    low = (rest - middle.astype(F32)).astype(BF16)
    parts = jnp.concatenate([high, middle, low], axis=1)
    by_row = lax.dot_general(
        parts, to_chip, (((0,), (0,)), ((), ())), preferred_element_type=F32
    )
    by_row = (by_row[:LANES] + by_row[LANES : 2 * LANES]) + by_row[2 * LANES :]
    at_lane = iota((LANES, ROWS), 0) == lane
    out_ref[...] = jnp.sum(jnp.where(at_lane, by_row, 0.0), axis=0, keepdims=True)
    last = iota((CHIPS, LANES), 1) == ((plan.first_lane() + plan.slots - 1) & (LANES - 1))
    flag_ref[0] = (jnp.max(jnp.where(last, back, 0.0)) > 0.0).astype(I32)


VMEM = pl.BlockSpec(memory_space=pltpu.VMEM)
SMEM = pl.BlockSpec(memory_space=pltpu.SMEM)
HBM = pl.BlockSpec(memory_space=pltpu.HBM)


def shape(dims, dtype):
    return jax.ShapeDtypeStruct(dims, dtype)


def call(kernel, plan, name, **options):
    return pl.pallas_call(
        functools.partial(kernel, plan),
        compiler_params=pltpu.CompilerParams(vmem_limit_bytes=48 * 1024 * 1024),
        name=name,
        **options,
    )


def swap(plan, message):
    return lax.all_to_all(message, ("yx", "z"), split_axis=0, concat_axis=0, tiled=True)


def owner_path(plan, embeddings, cluster_ids):
    message, where = call(
        send_kernel,
        plan,
        "send",
        out_shape=(shape((plan.held, WIDTH), BF16), shape((8, ROWS), I32)),
        in_specs=[HBM, HBM],
        out_specs=(VMEM, VMEM),
        scratch_shapes=[
            pltpu.VMEM((1, ROWS), I32),
            pltpu.VMEM((ROWS, WIDTH), BF16),
            pltpu.SemaphoreType.DMA((2,)),
        ],
    )(cluster_ids.reshape(1, ROWS), embeddings)
    held = swap(plan, message)
    packed, tags, pos = call(
        compact_kernel,
        plan,
        "compact",
        out_shape=(
            shape((plan.capacity + plan.tail, WIDTH), BF16),
            shape((plan.capacity, LANES), BF16),
            shape((8, plan.held), I32),
        ),
        in_specs=[VMEM],
        out_specs=(VMEM, VMEM, VMEM),
        scratch_shapes=[
            pltpu.VMEM((plan.held + plan.window, WIDTH), BF16),
            pltpu.VMEM((plan.held + plan.window, LANES), BF16),
        ],
    )(held)
    other = lax.ppermute(packed, "core", [(0, 1), (1, 0)])
    part = call(
        own_kernel,
        plan,
        "score_own",
        out_shape=shape((plan.capacity, LANES), F32),
        in_specs=[VMEM, VMEM],
        out_specs=VMEM,
        cost_estimate=pl.CostEstimate(
            flops=2 * plan.capacity**2 * WIDTH,
            bytes_accessed=2 * plan.capacity * WIDTH,
            transcendentals=0,
        ),
    )(packed, tags)
    best = call(
        other_kernel,
        plan,
        "score_other",
        out_shape=shape((CHIPS, LANES), F32),
        in_specs=[VMEM] * 5,
        out_specs=VMEM,
    )(pos, packed, tags, other, part)
    back = swap(plan, best)
    answer, flag = call(
        answer_kernel,
        plan,
        "answer",
        out_shape=(shape((1, ROWS), F32), shape((1,), I32)),
        in_specs=[VMEM, VMEM],
        out_specs=(VMEM, SMEM),
    )(where, back)
    return answer.reshape(ROWS), flag[0]


def pair_max(left_rows, left_ids, left_pos, right_rows, right_ids, right_pos):
    left_total, width = left_rows.shape
    left_step = min(512, left_total)
    left_count = left_total // left_step

    def left_turn(carry, left_tuple):
        part_rows, part_ids, part_pos = left_tuple
        scores = lax.dot_general(
            part_rows, right_rows, (((1,), (1,)), ((), ())), preferred_element_type=F32
        )
        matches = (
            (part_ids[:, None] == right_ids[None, :])
            & (part_ids[:, None] >= 0)
            & (part_pos[:, None] != right_pos[None, :])
        )
        return carry, jnp.max(jnp.where(matches, scores, -1.0), axis=1)

    _, row_best = lax.scan(
        left_turn,
        0,
        (
            left_rows.reshape(left_count, left_step, width),
            left_ids.reshape(left_count, left_step),
            left_pos.reshape(left_count, left_step),
        ),
    )
    return row_best.reshape(-1)


def gather(piece):
    copies = jnp.broadcast_to(piece[None], (4, *piece.shape))
    whole = lax.all_to_all(copies, "z", split_axis=0, concat_axis=0, tiled=True)
    return whole.reshape(-1, *piece.shape[1:])


def any_path(embeddings, cluster_ids):
    axes = ("yx", "core")
    widened = embeddings.astype(F32)
    normed = (
        widened * lax.rsqrt(jnp.sum(widened * widened, axis=1, keepdims=True) + 1e-06)
    ).astype(BF16)
    owner_group = cluster_ids // CL_GRP
    one_hot = (owner_group[:, None] == jnp.arange(GROUPS, dtype=I32)[None, :]).astype(I32)
    slot_index = jnp.sum(jnp.cumsum(one_hot, axis=0) * one_hot, axis=1) - 1
    flat_slot = owner_group * GROUP_CAP + slot_index
    total = GROUPS * GROUP_CAP
    placement = jnp.arange(total, dtype=I32)[:, None] == flat_slot[None, :]
    outgoing = jnp.dot(placement.astype(BF16), normed, preferred_element_type=F32).astype(BF16)
    outgoing = outgoing.reshape(GROUPS, GROUP_CAP, WIDTH)
    outgoing_ids = jnp.max(jnp.where(placement, cluster_ids[None, :], -1), axis=1)
    outgoing_ids = outgoing_ids.reshape(GROUPS, GROUP_CAP)
    received = lax.all_to_all(outgoing, axes, 0, 0, tiled=True).reshape(total, WIDTH)
    received_ids = lax.all_to_all(outgoing_ids, axes, 0, 0, tiled=True).reshape(total)
    own_pos = jnp.arange(total, dtype=I32) + lax.axis_index("z") * total
    piece_rows = gather(received)
    piece_ids = gather(received_ids)
    piece_pos = jnp.arange(piece_rows.shape[0], dtype=I32)
    best = pair_max(received, received_ids, own_pos, piece_rows, piece_ids, piece_pos)
    best = jnp.maximum(best, -1.0)
    returned = lax.all_to_all(best.reshape(GROUPS, GROUP_CAP), axes, 0, 0, tiled=True)
    return jnp.max(jnp.where(placement, returned.reshape(total)[:, None], -2.0), axis=0)


def unless_done(path, embeddings, cluster_ids, answer, flag):
    def turn(state):
        rows, ids, _, _ = state
        return rows, ids, path(rows, ids), jnp.int32(0)

    embeddings, cluster_ids, answer, flag = lax.optimization_barrier(
        (embeddings, cluster_ids, answer, flag)
    )
    state = (embeddings, cluster_ids, answer, flag)
    return lax.while_loop(lambda state: state[3] > 0, turn, state)[2]


def body(embeddings, cluster_ids):
    def roomy(rows, ids):
        return unless_done(any_path, rows, ids, *owner_path(ROOMY, rows, ids))

    return unless_done(
        roomy, embeddings, cluster_ids, *owner_path(TIGHT, embeddings, cluster_ids)
    )


def solution(mesh):
    chips = Mesh(np.asarray(mesh.devices).reshape(16, 2, 4), ("yx", "core", "z"))
    axes = ("yx", "core", "z")
    return jax.shard_map(
        body, mesh=chips, in_specs=(P(axes, None), P(axes)), out_specs=P(axes), check_vma=False
    )
```
